256 devices in a mesh: blk: 32 (over x_lo, z, core), uly: 8 (over y, x_hi).
Axes of the slice: x: 4 (x_hi: 2, x_lo: 2; x = x_hi * 2 + x_lo), y: 4, z: 8, core: 2. Of those that a mesh axis runs over, the one named last changes fastest.
Arguments:
- joint_qkv: bfloat16 [16384, 3, 3072], P(('blk', 'uly')), may hold values from -40 to 40
- text_count: int32 [1], replicated, may hold values from 1 to 512
- region_ids: int32 [16384], P('blk'), may hold values from 0 to 4
- region_identity: int32 [4], replicated, may hold values from 0 to 3, each once
- id_feats: bfloat16 [4, 256, 3072], P(None, 'blk'), may hold values from -6 to 6
- resample_mix: bfloat16 [32, 256], P(None, 'blk'), may hold values from -0.375 to 0.375
- latents: bfloat16 [32, 3072], replicated, may hold values from -6 to 6
- id_gain: float32 [3072], replicated, may hold values from 0.25 to 1.75
- id_kv_weight: bfloat16 [3072, 2, 3072], P(None, None, 'uly'), may hold values from -0.109375 to 0.109375
- out_weight: bfloat16 [3072, 3072], P('uly'), may hold values from -0.109375 to 0.109375
Outputs:
- output: bfloat16 [16384, 3072], P(('blk', 'uly'))
The draws below stay inside these ranges and needn't reach their ends.
Inputs may be any that keep to these rules, and one draw needn't show every extreme that they name: `region_identity`: A permutation of 0 to 3.
All inputs are finite; a program needn't handle non-finite values.
Results may differ from the reference program's by a relative error of at most 0.0095.
Values may be sent and summed in bfloat16 or wider, within the bound.
No kernel may reach another device: no remote copies, remote signals or barrier semaphores. Data moves between devices by JAX's collectives and lax.ppermute only.
A program may use at most 128 MiB of HBM per device.

```python
import math
import jax
import jax.numpy as jnp
from jax import lax

HEADS = 24
HEAD = 128
D = 3072
TXT = 512
SUBJ = 4
IDTOK = 32
SEQ = 16384
NFEAT = 256


def draw_joint_qkv(key, part):
    key = jax.random.fold_in(key, 11)
    width = HEADS * HEAD
    first = jax.random.fold_in(key, 0)
    base = jax.random.normal(first, (SEQ, 3, width), jnp.float32)
    spread = jnp.array([1.75, 1.75, 1.0], jnp.float32)[None, :, None]
    return jnp.clip(base * spread, -10.0, 10.0).astype(jnp.bfloat16)


def plant(values, key, low, largest):
    extent = values.shape
    index_at = [jax.random.randint(jax.random.fold_in(key, axis), (), 0, extent[axis]) for axis in range(len(extent))]
    values = values.at[tuple(index_at)].set(low)
    longest = extent.index(max(extent))
    index_at[longest] = (index_at[longest] + 1) % extent[longest]
    return values.at[tuple(index_at)].set(largest)


def shard_levels(own_key, shape, cuts, least, largest):
    level = 1.0
    for axis_at, parts in cuts:
        steps = jax.random.uniform(jax.random.fold_in(jax.random.fold_in(own_key, 6), axis_at), (parts,), jnp.float32, least / len(cuts), largest / len(cuts))
        level = level * jnp.repeat(jnp.exp(steps), shape[axis_at] // parts).reshape((-1,) + (1,) * (len(shape) - 1 - axis_at))
    return level


def bell_draw(rng, extent, scale, limit, cuts=(), kind=jnp.bfloat16):
    level = shard_levels(rng, extent, cuts, -0.22, 0.18) if cuts else 1.0
    entries = jax.random.normal(rng, extent, jnp.float32) * scale * level
    return jnp.minimum(jnp.maximum(entries, -limit), limit).astype(kind)


def setup_inputs(seed: int = 0) -> dict:
    key_list = jax.random.split(jax.random.key(seed), 11)
    joint_qkv = draw_joint_qkv(jax.random.fold_in(key_list[10], 71), 0)
    text_count = jax.random.randint(key_list[1], (1,), 1, TXT + 1).astype(jnp.int32)
    region_ids = plant(jax.random.randint(key_list[2], (SEQ,), 0, 5), jax.random.fold_in(key_list[2], 1), 0, 4).astype(jnp.int32)
    region_identity = jax.random.permutation(key_list[3], SUBJ).astype(jnp.int32)
    id_feats = bell_draw(key_list[4], (SUBJ, NFEAT, D), 1.0, 6.0, ((1, 32),))
    resample_mix = bell_draw(key_list[5], (IDTOK, NFEAT), NFEAT ** -0.5, 0.375, ((1, 32),))
    latents = bell_draw(key_list[6], (IDTOK, D), 1.0, 6.0)
    id_gain = jnp.clip(1.0 + 0.15 * jax.random.normal(key_list[7], (D,), jnp.float32), 0.25, 1.75)
    id_kv_weight = bell_draw(key_list[8], (D, 2, D), D ** -0.5, 0.109375, ((2, 8),))
    out_weight = bell_draw(key_list[9], (D, D), D ** -0.5, 0.109375, ((0, 8),))
    return dict(joint_qkv=joint_qkv, text_count=text_count, region_ids=region_ids, region_identity=region_identity, id_feats=id_feats, resample_mix=resample_mix, latents=latents, id_gain=id_gain, id_kv_weight=id_kv_weight, out_weight=out_weight)


def normalize(summed, id_gain):
    mean_square = lax.optimization_barrier(jnp.mean(summed * summed, axis=-1, keepdims=True))
    return (summed * lax.rsqrt(mean_square + 1e-06) * id_gain).astype(jnp.bfloat16)

def reference(joint_qkv, text_count, region_ids, region_identity, id_feats, resample_mix, latents, id_gain, id_kv_weight, out_weight):
    width = HEADS * HEAD
    pooled = jnp.einsum('jf,sfd->sjd', resample_mix.astype(jnp.float32), id_feats.astype(jnp.float32))
    summed = latents.astype(jnp.float32)[None] + pooled
    id_tokens = normalize(summed, id_gain).reshape(SUBJ * IDTOK, width)
    id_kv = jnp.einsum('nd,dce->nce', id_tokens.astype(jnp.float32), id_kv_weight.astype(jnp.float32)).astype(jnp.bfloat16)
    id_keys = id_kv[:, 0].reshape(SUBJ * IDTOK, HEADS, HEAD).astype(jnp.float32)
    id_values = id_kv[:, 1].reshape(SUBJ * IDTOK, HEADS, HEAD).astype(jnp.float32)
    positions = jnp.arange(SEQ, dtype=jnp.int32)
    usable = (positions >= TXT) | (positions < text_count[0])
    keys_all = joint_qkv[:, 1].reshape(SEQ, HEADS, HEAD).astype(jnp.float32)
    values_all = joint_qkv[:, 2].reshape(SEQ, HEADS, HEAD).astype(jnp.float32)
    score_scale = 1.0 / math.sqrt(HEAD)
    block_rows = math.gcd(SEQ, 256)
    key_subject = jnp.arange(SUBJ * IDTOK, dtype=jnp.int32) // IDTOK

    def attend_block(offset):
        queries = lax.dynamic_slice_in_dim(joint_qkv, offset, block_rows, 0)[:, 0]
        queries = queries.reshape(block_rows, HEADS, HEAD).astype(jnp.float32)
        scores = jnp.einsum('qhe,khe->hqk', queries, keys_all) * score_scale
        scores = jnp.where(usable[None, None, :], scores, -1e+30)
        peak = lax.optimization_barrier(jnp.max(scores, axis=-1, keepdims=True))
        exponent = jnp.exp(scores - peak)
        totals = lax.optimization_barrier(jnp.sum(exponent, axis=-1))
        weights = lax.optimization_barrier(exponent.astype(jnp.bfloat16)).astype(jnp.float32)
        joint = jnp.einsum('hqk,khe->qhe', weights, values_all) / jnp.transpose(totals)[:, :, None]
        region = lax.dynamic_slice_in_dim(region_ids, offset, block_rows, 0)
        block_pos = offset + jnp.arange(block_rows, dtype=jnp.int32)
        has_id = (region > 0) & (block_pos >= TXT)
        subject = jnp.zeros((block_rows,), jnp.int32)
        for which in range(SUBJ):
            subject = subject + jnp.where(region == which + 1, region_identity[which], 0)
        matches = (key_subject[None, :] == subject[:, None]) & has_id[:, None]
        id_scores = jnp.einsum('qhe,nhe->hqn', queries, id_keys) * score_scale
        id_scores = jnp.where(matches[None], id_scores, -1e+30)
        id_peak = lax.optimization_barrier(jnp.max(id_scores, axis=-1, keepdims=True))
        id_expo = jnp.exp(id_scores - id_peak) * matches[None].astype(jnp.float32)
        id_totals = lax.optimization_barrier(jnp.sum(id_expo, axis=-1)) + jnp.where(has_id, 0.0, 1.0)[None, :]
        id_weights = lax.optimization_barrier(id_expo.astype(jnp.bfloat16)).astype(jnp.float32)
        idpart = jnp.einsum('hqn,nhe->qhe', id_weights, id_values) / jnp.transpose(id_totals)[:, :, None]
        mixed_heads = (joint + idpart).reshape(block_rows, width).astype(jnp.bfloat16)
        return jnp.dot(mixed_heads, out_weight, preferred_element_type=jnp.float32).astype(jnp.bfloat16)
    starts = jnp.arange(SEQ // block_rows, dtype=jnp.int32) * block_rows
    return lax.map(attend_block, starts).reshape(SEQ, width)
```

```python
import functools
import math

import jax
import jax.numpy as jnp
from jax import lax
from jax.experimental import pallas as pl
from jax.experimental.pallas import tpu as pltpu
from jax.sharding import Mesh
from jax.sharding import PartitionSpec as P

HEAD = 128
TXT = 512
SUBJ = 4
IDTOK = 32
SCALE2 = math.log2(math.e) / math.sqrt(HEAD)
LIMIT = 96.0
QT = 1024
SUB = 256
bf16 = jnp.bfloat16
f32 = jnp.float32
TRANSPOSED = (((1,), (1,)), ((), ()))
BLK = ("xl", "z", "c")
ULY = ("y", "xh")
SWAP = [(0, 1), (1, 0)]


def attn_kernel(count, first, last, *refs):
    refs = list(refs)
    usable = refs.pop(0)
    flag_in = None if first else refs.pop(0)
    q_ref = refs.pop(0)
    k_refs = [refs.pop(0) for _ in range(count)]
    v_refs = [refs.pop(0) for _ in range(count)]
    acc_in = None if first else refs.pop(0)
    if last:
        sums_ref, lr_ref, vx, longest, acc_ref = refs
    else:
        acc_ref, flag_ref, vx, longest = refs
    head = pl.program_id(0)
    tile = pl.program_id(1)
    keys = [r.shape[0] for r in k_refs]

    @pl.when(tile == 0)
    def _():
        best = jnp.float32(0)
        ones = jnp.ones((HEAD, HEAD), bf16)
        at = 0
        for i in range(count):
            k = k_refs[i][...].astype(f32)
            square = jnp.dot((k * k).astype(bf16), ones, preferred_element_type=f32)
            best = jnp.maximum(best, jnp.max(square))
            rows = lax.broadcasted_iota(jnp.int32, (keys[i], HEAD), 0)
            cols = lax.broadcasted_iota(jnp.int32, (keys[i], HEAD), 1)
            ok = rows < usable[i]
            vx[at : at + keys[i], 0:HEAD] = jnp.where(ok, v_refs[i][...].astype(f32), 0.0).astype(bf16)
            vx[at : at + keys[i], HEAD : 2 * HEAD] = jnp.where(ok & (cols < 64), 1.0, 0.0).astype(bf16)
            at += keys[i]
        longest[0] = best

    rows_here = q_ref.shape[0]
    q = q_ref[...].astype(f32) * SCALE2
    square = jnp.dot((q * q).astype(bf16), jnp.ones((HEAD, HEAD), bf16), preferred_element_type=f32)
    fast = jnp.max(square) * longest[0] * 1.05 <= LIMIT * LIMIT
    if not first:
        fast = fast & (flag_in[head, tile] == 0)
    if not last:
        flag_ref[head, tile] = jnp.where(fast, 0, 1)
    q_high = q.astype(bf16)
    q_low = (q - q_high.astype(f32)).astype(bf16)
    q_both = jnp.concatenate([q_high, q_low], axis=1)

    @pl.when(fast)
    def _():
        for start in range(0, rows_here, SUB):
            total = None if first else acc_in[start : start + SUB, :]
            at = 0
            for i in range(count):
                k = k_refs[i][...]
                kk = jnp.concatenate([k, k], axis=1)
                scores = lax.dot_general(
                    q_both[start : start + SUB], kk, TRANSPOSED, preferred_element_type=f32
                )
                p = jnp.exp2(scores).astype(bf16)
                part = jnp.dot(p, vx[at : at + keys[i], :], preferred_element_type=f32)
                total = part if total is None else total + part
                at += keys[i]
            acc_ref[start : start + SUB, :] = total

    @pl.when(jnp.logical_not(fast))
    def _():
        lane = lax.broadcasted_iota(jnp.int32, (rows_here, 2 * HEAD), 1)
        total = jnp.zeros((rows_here, 2 * HEAD), f32) if first else acc_in[...]
        at = 0
        for i in range(count):
            k = k_refs[i][...]
            kk = jnp.concatenate([k, k], axis=1)
            scores = lax.dot_general(q_both, kk, TRANSPOSED, preferred_element_type=f32)
            scores = jnp.where(lax.broadcasted_iota(jnp.int32, scores.shape, 1) < usable[i], scores, -1e30)
            peak = jnp.max(scores, axis=1, keepdims=True)
            old = jnp.where(total[:, HEAD : HEAD + 1] > 0, total[:, 2 * HEAD - 1 : 2 * HEAD], -1e30)
            new = jnp.maximum(old, peak)
            p = jnp.exp2(scores - new).astype(bf16)
            part = jnp.dot(p, vx[at : at + keys[i], :], preferred_element_type=f32)
            total = jnp.where(lane < 192, total * jnp.exp2(old - new) + part, new)
            at += keys[i]
        acc_ref[...] = total

    if last:
        sums_ref[...] = acc_ref[:, 0:HEAD].astype(bf16)
        turned = acc_ref[:, HEAD : 2 * HEAD].T
        lr_ref[0:1, :] = turned[0:1, :]
        lr_ref[1:2, :] = turned[HEAD - 1 : HEAD, :]


def attend(usable, flag, q, shards, acc, last=False):
    count, first = len(shards), acc is None
    rows = q.shape[0]
    tiles = rows // QT
    heads = q.shape[1] // HEAD
    smem = pl.BlockSpec(memory_space=pltpu.SMEM)
    acc_block = pl.BlockSpec((None, QT, 2 * HEAD), lambda h, t: (h, t, 0))
    in_specs, args = [smem], [usable]
    if not first:
        in_specs.append(smem)
        args.append(flag)
    in_specs.append(pl.BlockSpec((QT, HEAD), lambda h, t: (t, h)))
    args.append(q)
    for shift in (0, heads):
        for kv in shards:
            in_specs.append(pl.BlockSpec((kv.shape[0], HEAD), lambda h, t, s=shift: (0, s + h)))
            args.append(kv)
    if not first:
        in_specs.append(acc_block)
        args.append(acc)
    total = sum(kv.shape[0] for kv in shards)
    scratch = [pltpu.VMEM((total, 2 * HEAD), bf16), pltpu.SMEM((1,), f32)]
    if last:
        out_specs = [
            pl.BlockSpec((QT, HEAD), lambda h, t: (t, h)),
            pl.BlockSpec((None, 2, QT), lambda h, t: (h, 0, t)),
        ]
        out_shape = [
            jax.ShapeDtypeStruct((rows, heads * HEAD), bf16),
            jax.ShapeDtypeStruct((heads, 2, rows), f32),
        ]
        scratch.append(pltpu.VMEM((QT, 2 * HEAD), f32))
    else:
        out_specs = [acc_block, smem]
        out_shape = [
            jax.ShapeDtypeStruct((heads, rows, 2 * HEAD), f32),
            jax.ShapeDtypeStruct((heads, tiles), jnp.int32),
        ]
    return pl.pallas_call(
        functools.partial(attn_kernel, count, first, last),
        grid=(heads, tiles),
        in_specs=in_specs,
        out_specs=out_specs,
        out_shape=out_shape,
        scratch_shapes=scratch,
        cost_estimate=pl.CostEstimate(
            flops=heads * rows * total * 2048,
            bytes_accessed=12 * 2**20,
            transcendentals=heads * rows * total,
        ),
        compiler_params=pltpu.CompilerParams(vmem_limit_bytes=40 * 2**20),
    )(*args)


def id_kernel(q_ref, kv_ref, match_ref, out_ref):
    width = q_ref.shape[1]
    match = match_ref[...]
    lacking = 1.0 - jnp.max(match, axis=1, keepdims=True)
    for h in range(width // HEAD):
        cols = slice(h * HEAD, (h + 1) * HEAD)
        scores = lax.dot_general(
            q_ref[:, cols], kv_ref[:, cols], TRANSPOSED, preferred_element_type=f32
        ) * (1.0 / math.sqrt(HEAD))
        scores = jnp.where(match > 0, scores, -1e30)
        peak = jnp.max(scores, axis=1, keepdims=True)
        expo = jnp.exp(scores - peak) * match
        totals = jnp.sum(expo, axis=1, keepdims=True) + lacking
        v = kv_ref[:, width + h * HEAD : width + (h + 1) * HEAD]
        out_ref[:, cols] = jnp.dot(expo.astype(bf16), v, preferred_element_type=f32) / totals


def id_attend(q, id_kv, match):
    return pl.pallas_call(
        id_kernel,
        out_shape=jax.ShapeDtypeStruct(q.shape, f32),
        compiler_params=pltpu.CompilerParams(vmem_limit_bytes=32 * 2**20),
    )(q, id_kv, match)


def combine_kernel(place, keep, recv, lr_own, lr_core, lr_x, lr_far, id_ref, out_ref):
    slot = pl.program_id(0)
    rows = keep.shape[0]
    refs = [r[1:2, :] for r in (lr_own, lr_core, lr_x, lr_far)]
    sums = [r[0:1, :] for r in (lr_own, lr_core, lr_x, lr_far)]
    top = functools.reduce(jnp.maximum, refs)
    weight = [jnp.exp2(r - top) for r in refs]
    total = sum(w * s for w, s in zip(weight, sums))

    def column(row):
        return jnp.broadcast_to(row, (HEAD, rows)).T

    value = keep[...].astype(f32) * column(weight[0] / total)
    value = value + recv[...].astype(f32) * column(weight[1] / total)

    @pl.when(slot == 0)
    def _():
        out_ref[...] = (value + id_ref[...]).astype(bf16)

    @pl.when(slot == 1)
    def _():
        out_ref[...] = value.astype(bf16)


def combine(place, sums, recv, lr, lr_core, lr_x, lr_far, idpart):
    tokens, width = idpart.shape
    heads = width // HEAD
    data = pl.BlockSpec((tokens, HEAD), lambda s, h, p: (s, h))
    near = pl.BlockSpec((None, 2, tokens), lambda s, h, p: (h, 0, s))
    cross = pl.BlockSpec((None, 2, tokens), lambda s, h, p: (h, 0, 1 - s))
    return pl.pallas_call(
        combine_kernel,
        grid_spec=pltpu.PrefetchScalarGridSpec(
            num_scalar_prefetch=1,
            grid=(2, heads),
            in_specs=[
                data,
                data,
                near,
                near,
                cross,
                cross,
                pl.BlockSpec((tokens, HEAD), lambda s, h, p: (0, h)),
            ],
            out_specs=pl.BlockSpec((None, tokens, HEAD), lambda s, h, p: ((p[0] + s) % 2, 0, h)),
        ),
        out_shape=jax.ShapeDtypeStruct((2, tokens, width), bf16),
        compiler_params=pltpu.CompilerParams(vmem_limit_bytes=32 * 2**20),
    )(place, sums, recv, lr, lr_core, lr_x, lr_far, idpart)


def normalize(summed, mean_square, id_gain):
    return (summed * lax.rsqrt(mean_square + 1e-06) * id_gain).astype(bf16)


def identity_kv(id_feats, resample_mix, latents, id_gain, id_kv_weight, number):
    width_here = id_kv_weight.shape[2]
    width = id_kv_weight.shape[0]
    here = id_feats.shape[1]
    groups = width // width_here
    feats = lax.dynamic_slice_in_dim(id_feats, number * width_here, width_here, 2)
    feats = feats.reshape(SUBJ * here, width_here)
    mix_row = jnp.pad(resample_mix.reshape(1, IDTOK * here), ((0, 15), (0, width_here - IDTOK * here)))
    packed = lax.all_gather(jnp.concatenate([feats, mix_row], axis=0), BLK, axis=0)
    shards = packed.shape[0]
    feats_all = packed[:, : SUBJ * here].reshape(shards, SUBJ, here, width_here)
    mix_all = packed[:, SUBJ * here, : IDTOK * here].reshape(shards, IDTOK, here)
    pooled = jnp.einsum("bjf,bsfd->sjd", mix_all, feats_all, preferred_element_type=f32)
    own = lax.dynamic_slice_in_dim(latents, number * width_here, width_here, 1).astype(f32)
    summed = (own[None] + pooled).reshape(SUBJ * IDTOK, width_here)
    summed = lax.all_gather(summed, ULY, axis=0)
    mean_square = jnp.sum(summed * summed, axis=(0, 2), keepdims=True) / width
    tokens = normalize(summed, mean_square, id_gain.reshape(groups, 1, width_here))
    tokens = tokens.transpose(1, 0, 2).reshape(SUBJ * IDTOK, width)
    keys = jnp.dot(tokens, id_kv_weight[:, 0], preferred_element_type=f32)
    values = jnp.dot(tokens, id_kv_weight[:, 1], preferred_element_type=f32)
    return jnp.concatenate([keys, values], axis=1).astype(bf16)


def on_device(
    joint_qkv,
    text_count,
    region_ids,
    region_identity,
    id_feats,
    resample_mix,
    latents,
    id_gain,
    id_kv_weight,
    out_weight,
):
    z_size = lax.axis_size("z")
    y_size = lax.axis_size("y")
    uly = y_size * lax.axis_size("xh")
    tok_dev = joint_qkv.shape[0]
    tok_blk = tok_dev * uly
    width = joint_qkv.shape[2]
    here = width // uly
    my_xl, my_z, my_c = lax.axis_index("xl"), lax.axis_index("z"), lax.axis_index("c")
    number = lax.axis_index(ULY)

    by_group = joint_qkv.reshape(tok_dev, 3, uly, here)
    kv_out = jnp.concatenate([by_group[:, 1], by_group[:, 2]], axis=-1).transpose(1, 0, 2)
    q_out = by_group[:, 0].transpose(1, 0, 2)
    kv = lax.all_to_all(kv_out, ULY, 0, 0, tiled=True).reshape(tok_blk, 2 * here)
    q_own = lax.all_to_all(q_out, ULY, 0, 0, tiled=True).reshape(tok_blk, here)
    q_x = lax.ppermute(q_own, "xl", SWAP)
    q_pair = jnp.concatenate([q_own, q_x], axis=0)
    queries = jnp.concatenate([q_pair, lax.ppermute(q_pair, "c", SWAP)], axis=0)

    def limits(origin, halves):
        text_here = (my_xl == 0) & (my_c == 0) & (origin % z_size == 0)
        used = jnp.where(text_here, text_count[0], tok_blk)
        if not halves:
            return [used]
        half = tok_blk // 2
        return [jnp.minimum(used, half), jnp.clip(used - half, 0, half)]

    right = [(i, (i + 1) % z_size) for i in range(z_size)]
    left = [(i, (i - 1) % z_size) for i in range(z_size)]
    up, down = kv, kv
    steps = []
    held, marks = [kv], limits(my_z, False)
    for step in range(1, z_size // 2):
        up = lax.ppermute(up, "z", right)
        down = lax.ppermute(down, "z", left)
        held += [up, down]
        marks += limits(my_z - step + z_size, False) + limits(my_z + step, False)
        steps.append((held, marks))
        held, marks = [], []
    half = tok_blk // 2
    steps.append(
        (
            [lax.ppermute(up[:half], "z", right), lax.ppermute(down[half:], "z", left)],
            limits(my_z + z_size // 2, True),
        )
    )
    acc, flag = None, None
    for at, (held, marks) in enumerate(steps):
        usable = jnp.stack(marks).astype(jnp.int32)
        acc, flag = attend(usable, flag, queries, held, acc, last=at == len(steps) - 1)
    sums, lr = acc, flag

    id_kv = identity_kv(id_feats, resample_mix, latents, id_gain, id_kv_weight, number)
    block = (my_xl * z_size + my_z) * 2 + my_c
    position = block * tok_blk + jnp.arange(tok_blk, dtype=jnp.int32)
    has_id = (region_ids > 0) & (position >= TXT)
    subject = jnp.zeros((tok_blk,), jnp.int32)
    for which in range(SUBJ):
        subject = subject + jnp.where(region_ids == which + 1, region_identity[which], 0)
    key_subject = jnp.arange(SUBJ * IDTOK, dtype=jnp.int32) // IDTOK
    match = ((key_subject[None, :] == subject[:, None]) & has_id[:, None]).astype(f32)
    idpart = id_attend(q_own, id_kv, match)

    pair = 2 * tok_blk
    recv = lax.ppermute(sums[pair:], "c", SWAP)
    lr_near, lr_send = lr[:, :, :pair], lr[:, :, pair:]
    lr_core = lax.ppermute(lr_send, "c", SWAP)
    lr_x = lax.ppermute(lr_near, "xl", SWAP)
    lr_far = lax.ppermute(lr_send, ("xl", "c"), [(i, 3 - i) for i in range(4)])
    mixed = combine(my_xl[None], sums, recv, lr, lr_core, lr_x, lr_far, idpart)

    quarter = tok_blk // y_size
    mixed = mixed.reshape(2 * y_size, quarter, here)
    mixed = lax.all_to_all(mixed, ("xl", "y"), 0, 0, tiled=True)
    mixed = mixed.reshape(2, y_size, quarter, here).astype(f32)
    mixed = (mixed[0] + mixed[1]).astype(bf16)
    mixed = mixed.transpose(1, 0, 2).reshape(quarter, y_size * here)

    weight = lax.all_gather(out_weight, "y", axis=0).reshape(y_size * here, width)
    product = jnp.dot(mixed, weight, preferred_element_type=f32)
    my_xh = lax.axis_index("xh")
    mine = lax.dynamic_slice_in_dim(product, my_xh * tok_dev, tok_dev, 0)
    other = lax.dynamic_slice_in_dim(product, (1 - my_xh) * tok_dev, tok_dev, 0)
    return (mine + lax.ppermute(other.astype(bf16), "xh", SWAP).astype(f32)).astype(bf16)


def solution(mesh):
    fine = Mesh(mesh.devices.reshape(2, 8, 2, 4, 2), BLK + ULY)
    placed = (
        P(BLK + ULY, None, None),
        P(),
        P(BLK),
        P(),
        P(None, BLK, None),
        P(None, BLK),
        P(),
        P(),
        P(None, None, ULY),
        P(ULY, None),
    )
    return jax.shard_map(
        on_device, mesh=fine, in_specs=placed, out_specs=P(BLK + ULY, None), check_vma=False
    )
```

```python
import functools
import math

import jax
import jax.numpy as jnp
from jax import lax
from jax.experimental import pallas as pl
from jax.experimental.pallas import tpu as pltpu
from jax.sharding import Mesh
from jax.sharding import PartitionSpec as P

HEAD = 128
TXT = 512
SUBJ = 4
IDTOK = 32
SCALE2 = math.log2(math.e) / math.sqrt(HEAD)
QT = 2048
SUB = 256
bf16 = jnp.bfloat16
f32 = jnp.float32
TRANSPOSED = (((1,), (1,)), ((), ()))
BLK = ("xl", "z", "c")
ULY = ("y", "xh")
SWAP = [(0, 1), (1, 0)]


def usable(count, mark):
    z, offset, size = mark
    text = (lax.axis_index("xl") == 0) & (lax.axis_index("c") == 0) & (lax.axis_index("z") == z)
    return jnp.where(text, jnp.clip(count - offset, 0, size), size)


def attn_kernel(marks, marks_all, first, last, sub, *refs):
    refs = list(refs)
    count = len(marks)
    text_count, q_ref = refs.pop(0), refs.pop(0)
    k_refs = [refs.pop(0) for _ in range(count)]
    v_refs = [refs.pop(0) for _ in range(count)]
    acc_in = None if first else refs.pop(0)
    if last:
        *shards, sums_ref, lr_ref, ones, acc_ref, k_buf, v_buf, top_ref = refs
    else:
        acc_ref, ones = refs
    head = pl.program_id(0)
    rows_here = q_ref.shape[0]
    keys = [r.shape[0] for r in k_refs]

    @pl.when((head == 0) & (pl.program_id(1) == 0))
    def _():
        at = 0
        for i in range(count):
            rows = lax.broadcasted_iota(jnp.int32, (keys[i], HEAD), 0)
            ones[at : at + keys[i], :] = jnp.where(rows < usable(text_count[0], marks[i]), 1.0, 0.0).astype(bf16)
            at += keys[i]

    def split(q):
        q = q.astype(f32) * SCALE2
        high = q.astype(bf16)
        return jnp.concatenate([high, (q - high.astype(f32)).astype(bf16)], axis=1)

    def score(q, k):
        return lax.dot_general(q, jnp.concatenate([k, k], axis=1), TRANSPOSED, preferred_element_type=f32)

    for start in range(0, rows_here, sub):
        total = None if first else acc_in[start : start + sub, :]
        q = split(q_ref[start : start + sub, :])
        at = 0
        for i in range(count):
            p = jnp.exp2(score(q, k_refs[i][...])).astype(bf16)
            v = jnp.concatenate([v_refs[i][...], ones[at : at + keys[i], :]], axis=1)
            part = jnp.dot(p, v, preferred_element_type=f32)
            total = part if total is None else total + part
            at += keys[i]
        acc_ref[start : start + sub, :] = total

    if last:
        sums_ref[...] = acc_ref[:, 0:HEAD].astype(bf16)
        totals = acc_ref[:, HEAD : 2 * HEAD].T[0:1, :]
        lr_ref[0:1, :] = totals
        lr_ref[1:2, :] = jnp.zeros_like(totals)
        good = jnp.min(jnp.where((totals >= 2.0**-60) & (totals <= 2.0**100), 1.0, 0.0)) > 0.5

        @pl.when(jnp.logical_not(good))
        def _():
            acc_ref[...] = jnp.zeros_like(acc_ref)
            top_ref[...] = jnp.full_like(top_ref, -1e30)
            for i, shard in enumerate(shards):
                here = slice(0, shard.shape[0])
                key_at = pl.multiple_of(head * HEAD, HEAD)
                value_at = pl.multiple_of(shard.shape[1] // 2 + head * HEAD, HEAD)
                pltpu.sync_copy(shard.at[:, pl.ds(key_at, HEAD)], k_buf.at[here, :])
                pltpu.sync_copy(shard.at[:, pl.ds(value_at, HEAD)], v_buf.at[here, :])
                for start in range(0, rows_here, sub):
                    part = slice(start, start + sub)
                    scores = score(split(q_ref[part, :]), k_buf[here, :])
                    key = lax.broadcasted_iota(jnp.int32, scores.shape, 1)
                    scores = jnp.where(key < usable(text_count[0], marks_all[i]), scores, -1e30)
                    old = top_ref[part, 0:1]
                    new = jnp.maximum(old, jnp.max(scores, axis=1, keepdims=True))
                    p = jnp.exp2(scores - new).astype(bf16)
                    v = v_buf[here, :]
                    v = jnp.concatenate([v, jnp.ones_like(v)], axis=1)
                    added = jnp.dot(p, v, preferred_element_type=f32)
                    acc_ref[part, :] = acc_ref[part, :] * jnp.exp2(old - new) + added
                    top_ref[part, :] = jnp.broadcast_to(new, (sub, HEAD))
            sums_ref[...] = acc_ref[:, 0:HEAD].astype(bf16)
            lr_ref[0:1, :] = acc_ref[:, HEAD : 2 * HEAD].T[0:1, :]
            lr_ref[1:2, :] = top_ref[...].T[0:1, :]


def attend(text_count, q, shards, acc, everything=None, tile=QT, sub=SUB):
    shards, marks = [kv for kv, _ in shards], [mark for _, mark in shards]
    first, last = acc is None, everything is not None
    marks_all = None
    rows = q.shape[0]
    heads = q.shape[1] // HEAD
    smem = pl.BlockSpec(memory_space=pltpu.SMEM)
    acc_block = pl.BlockSpec((None, tile, 2 * HEAD), lambda h, t: (h, t, 0))
    in_specs = [smem, pl.BlockSpec((tile, HEAD), lambda h, t: (t, h))]
    args = [text_count, q]
    for shift in (0, heads):
        for kv in shards:
            in_specs.append(pl.BlockSpec((kv.shape[0], HEAD), lambda h, t, s=shift: (0, s + h)))
            args.append(kv)
    if not first:
        in_specs.append(acc_block)
        args.append(acc)
    total = sum(kv.shape[0] for kv in shards)
    scratch = [pltpu.VMEM((total, HEAD), bf16)]
    if last:
        in_specs += [pl.BlockSpec(memory_space=pl.ANY)] * len(everything)
        args += [kv for kv, _ in everything]
        marks_all = [mark for _, mark in everything]
        out_specs = [
            pl.BlockSpec((tile, HEAD), lambda h, t: (t, h)),
            pl.BlockSpec((None, 2, tile), lambda h, t: (h, 0, t)),
        ]
        out_shape = [
            jax.ShapeDtypeStruct((rows, heads * HEAD), bf16),
            jax.ShapeDtypeStruct((heads, 2, rows), f32),
        ]
        keys = everything[0][0].shape[0]
        scratch += [
            pltpu.VMEM((tile, 2 * HEAD), f32),
            pltpu.VMEM((keys, HEAD), bf16),
            pltpu.VMEM((keys, HEAD), bf16),
            pltpu.VMEM((tile, HEAD), f32),
        ]
    else:
        out_specs = acc_block
        out_shape = jax.ShapeDtypeStruct((heads, rows, 2 * HEAD), f32)
    return pl.pallas_call(
        functools.partial(attn_kernel, marks, marks_all, first, last, sub),
        grid=(heads, rows // tile),
        in_specs=in_specs,
        out_specs=out_specs,
        out_shape=out_shape,
        scratch_shapes=scratch,
        cost_estimate=pl.CostEstimate(
            flops=heads * rows * total * 2048,
            bytes_accessed=12 * 2**20,
            transcendentals=heads * rows * total,
        ),
        compiler_params=pltpu.CompilerParams(vmem_limit_bytes=60 * 2**20),
    )(*args)


def id_kernel(q_ref, kv_ref, match_ref, out_ref):
    width = q_ref.shape[1]
    match = match_ref[...]
    lacking = 1.0 - jnp.max(match, axis=1, keepdims=True)
    for h in range(width // HEAD):
        cols = slice(h * HEAD, (h + 1) * HEAD)
        scores = lax.dot_general(
            q_ref[:, cols], kv_ref[:, cols], TRANSPOSED, preferred_element_type=f32
        ) * (1.0 / math.sqrt(HEAD))
        scores = jnp.where(match > 0, scores, -1e30)
        peak = jnp.max(scores, axis=1, keepdims=True)
        expo = jnp.exp(scores - peak) * match
        totals = jnp.sum(expo, axis=1, keepdims=True) + lacking
        v = kv_ref[:, width + h * HEAD : width + (h + 1) * HEAD]
        out_ref[:, cols] = jnp.dot(expo.astype(bf16), v, preferred_element_type=f32) / totals


def id_attend(q, id_kv, match):
    return pl.pallas_call(
        id_kernel,
        out_shape=jax.ShapeDtypeStruct(q.shape, f32),
        compiler_params=pltpu.CompilerParams(vmem_limit_bytes=32 * 2**20),
    )(q, id_kv, match)


def combine_kernel(keep, recv, lr_own, lr_core, lr_x, lr_far, id_ref, out_ref):
    slot = pl.program_id(0)
    tokens, width = keep.shape
    place = lax.rem(lax.axis_index("xl") + slot, 2)
    for h in range(width // HEAD):
        refs = [r[h, 1:2, :] for r in (lr_own, lr_core, lr_x, lr_far)]
        sums = [r[h, 0:1, :] for r in (lr_own, lr_core, lr_x, lr_far)]
        top = functools.reduce(jnp.maximum, refs)
        weight = [jnp.exp2(r - top) for r in refs]
        total = sum(w * s for w, s in zip(weight, sums))

        def column(row):
            return jnp.broadcast_to(row, (HEAD, tokens)).T

        cols = slice(h * HEAD, (h + 1) * HEAD)
        value = keep[:, cols].astype(f32) * column(weight[0] / total)
        value = value + recv[:, cols].astype(f32) * column(weight[1] / total)
        value = value + jnp.where(slot == 0, id_ref[:, cols], 0.0)
        out_ref[place, :, cols] = value.astype(bf16)


def combine(sums, recv, lr, lr_core, lr_x, lr_far, idpart):
    tokens, width = idpart.shape
    heads = width // HEAD
    data = pl.BlockSpec((tokens, width), lambda s: (s, 0))
    near = pl.BlockSpec((heads, 2, tokens), lambda s: (0, 0, s))
    cross = pl.BlockSpec((heads, 2, tokens), lambda s: (0, 0, 1 - s))
    return pl.pallas_call(
        combine_kernel,
        grid=(2,),
        in_specs=[data, data, near, near, cross, cross, pl.BlockSpec((tokens, width), lambda s: (0, 0))],
        out_specs=pl.BlockSpec((2, tokens, width), lambda s: (0, 0, 0)),
        out_shape=jax.ShapeDtypeStruct((2, tokens, width), bf16),
        compiler_params=pltpu.CompilerParams(vmem_limit_bytes=60 * 2**20),
    )(sums, recv, lr, lr_core, lr_x, lr_far, idpart)


def spread_kernel(text_count, qkv, out):
    rows, _, width = qkv.shape
    sizes = [lax.axis_size(a) for a in BLK + ULY]
    number = 0
    for axis, size in zip(BLK + ULY, sizes):
        number = number * size + lax.axis_index(axis)
    start = number * rows
    limit = jnp.where(start >= TXT, rows, jnp.clip(text_count[0] - start, 0, rows))
    for part in range(2):
        out[:, part * width : (part + 1) * width] = qkv[:, part, :]
    used = lax.broadcasted_iota(jnp.int32, (rows, width), 0) < limit
    out[:, 2 * width :] = jnp.where(used, qkv[:, 2, :].astype(f32), 0.0).astype(bf16)


def spread(text_count, joint_qkv, groups):
    rows, _, width = joint_qkv.shape
    here = width // groups
    return pl.pallas_call(
        spread_kernel,
        grid=(groups,),
        in_specs=[
            pl.BlockSpec(memory_space=pltpu.SMEM),
            pl.BlockSpec((rows, 3, here), lambda u: (0, 0, u)),
        ],
        out_specs=pl.BlockSpec((None, rows, 3 * here), lambda u: (u, 0, 0)),
        out_shape=jax.ShapeDtypeStruct((groups, rows, 3 * here), bf16),
    )(text_count, joint_qkv)


def normalize(summed, mean_square, id_gain):
    return (summed * lax.rsqrt(mean_square + 1e-06) * id_gain).astype(bf16)


def pack_features(id_feats, resample_mix, number, width_here):
    here = id_feats.shape[1]
    feats = lax.dynamic_slice_in_dim(id_feats, number * width_here, width_here, 2)
    feats = feats.reshape(SUBJ * here, width_here)
    mix_row = jnp.pad(resample_mix.reshape(1, IDTOK * here), ((0, 15), (0, width_here - IDTOK * here)))
    return jnp.concatenate([feats, mix_row], axis=0)


def gather_summed(packed, latents, number, here):
    shards, _, width_here = packed.shape
    feats_all = packed[:, : SUBJ * here].reshape(shards, SUBJ, here, width_here)
    mix_all = packed[:, SUBJ * here, : IDTOK * here].reshape(shards, IDTOK, here)
    pooled = jnp.einsum("bjf,bsfd->sjd", mix_all, feats_all, preferred_element_type=f32)
    own = lax.dynamic_slice_in_dim(latents, number * width_here, width_here, 1).astype(f32)
    summed = (own[None] + pooled).reshape(SUBJ * IDTOK, width_here)
    return lax.all_gather(summed, ULY, axis=0)


def identity_kv(summed, id_gain, id_kv_weight):
    width, _, width_here = id_kv_weight.shape
    groups = width // width_here
    mean_square = jnp.sum(summed * summed, axis=(0, 2), keepdims=True) / width
    tokens = normalize(summed, mean_square, id_gain.reshape(groups, 1, width_here))
    tokens = tokens.transpose(1, 0, 2).reshape(SUBJ * IDTOK, width)
    keys = jnp.dot(tokens, id_kv_weight[:, 0], preferred_element_type=f32)
    values = jnp.dot(tokens, id_kv_weight[:, 1], preferred_element_type=f32)
    return jnp.concatenate([keys, values], axis=1).astype(bf16)


def project_kernel(mixed, own, before, after, far_low, far_high, mine, other, product):
    y, xh = lax.axis_index("y"), lax.axis_index("xh")
    groups = mixed.shape[0] // 2

    def group(k):
        at = lax.rem(y + k, groups)
        return (mixed[at].astype(f32) + mixed[groups + at].astype(f32)).astype(bf16)

    far = group(2)
    half = far_low.shape[0]
    total = jnp.dot(group(0), own[...], preferred_element_type=f32)
    total += jnp.dot(group(1), after[...], preferred_element_type=f32)
    total += jnp.dot(group(3), before[...], preferred_element_type=f32)
    total += jnp.dot(far[:, :half], far_low[...], preferred_element_type=f32)
    total += jnp.dot(far[:, half:], far_high[...], preferred_element_type=f32)
    product[...] = total
    rows = mine.shape[0]
    mine[...] = product[pl.ds(pl.multiple_of(xh * rows, rows), rows), :]
    other[...] = product[pl.ds(pl.multiple_of((1 - xh) * rows, rows), rows), :].astype(bf16)


def project(mixed, weights):
    tokens, width = mixed.shape[1] // 2, weights[0].shape[1]
    tile = 512
    columns = [pl.BlockSpec((w.shape[0], tile), lambda n: (0, n)) for w in weights]
    out = pl.BlockSpec((tokens, tile), lambda n: (0, n))
    return pl.pallas_call(
        project_kernel,
        grid=(width // tile,),
        in_specs=[pl.BlockSpec(mixed.shape, lambda n: (0, 0, 0))] + columns,
        out_specs=[out, out],
        out_shape=[
            jax.ShapeDtypeStruct((tokens, width), f32),
            jax.ShapeDtypeStruct((tokens, width), bf16),
        ],
        scratch_shapes=[pltpu.VMEM((2 * tokens, tile), f32)],
        compiler_params=pltpu.CompilerParams(vmem_limit_bytes=60 * 2**20),
    )(mixed, *weights)


def on_device(
    joint_qkv,
    text_count,
    region_ids,
    region_identity,
    id_feats,
    resample_mix,
    latents,
    id_gain,
    id_kv_weight,
    out_weight,
):
    z_size = lax.axis_size("z")
    y_size = lax.axis_size("y")
    uly = y_size * lax.axis_size("xh")
    tok_dev = joint_qkv.shape[0]
    tok_blk = tok_dev * uly
    width = joint_qkv.shape[2]
    here = width // uly
    my_xl, my_z, my_c = lax.axis_index("xl"), lax.axis_index("z"), lax.axis_index("c")
    number = lax.axis_index(ULY)

    block = (my_xl * z_size + my_z) * 2 + my_c
    features = pack_features(id_feats, resample_mix, number, here)
    features, joint_qkv = lax.optimization_barrier((features, joint_qkv))
    packed = lax.all_gather(features, BLK, axis=0)
    sent = spread(text_count, joint_qkv, uly)
    got = lax.all_to_all(sent, ULY, 0, 0, tiled=True).reshape(tok_blk, 3 * here)
    q_own, kv = got[:, :here], got[:, here:]
    q_x = lax.ppermute(q_own, "xl", SWAP)
    q_pair = jnp.concatenate([q_own, q_x], axis=0)
    queries = jnp.concatenate([q_pair, lax.ppermute(q_pair, "c", SWAP)], axis=0)

    around = lax.axis_size("y")
    onward = [(i, (i + 1) % around) for i in range(around)]
    backward = [(i, (i - 1) % around) for i in range(around)]
    before = lax.ppermute(out_weight, "y", onward)
    after = lax.ppermute(out_weight, "y", backward)
    far_low = lax.ppermute(before[: here // 2], "y", onward)
    far_high = lax.ppermute(after[here // 2 :], "y", backward)

    right = [(i, (i + 1) % z_size) for i in range(z_size)]
    left = [(i, (i - 1) % z_size) for i in range(z_size)]
    up, down = kv, kv
    half = tok_blk // 2
    first = (kv, (0, 0, tok_blk))
    steps = []
    for step in range(1, z_size // 2):
        up = lax.ppermute(up, "z", right)
        down = lax.ppermute(down, "z", left)
        steps.append([(up, (step, 0, tok_blk)), (down, (z_size - step, 0, tok_blk))])
    end = z_size // 2
    steps.append(
        [
            (lax.ppermute(up[:half], "z", right), (end, 0, half)),
            (lax.ppermute(down[half:], "z", left), (end, half, half)),
        ]
    )
    acc = attend(text_count, queries, [first], None)
    packed, acc = lax.optimization_barrier((packed, acc))
    summed = gather_summed(packed, latents, number, id_feats.shape[1])
    for held in steps[:-1]:
        acc = attend(text_count, queries, held, acc)
    id_kv = identity_kv(summed, id_gain, id_kv_weight)
    position = block * tok_blk + jnp.arange(tok_blk, dtype=jnp.int32)
    has_id = (region_ids > 0) & (position >= TXT)
    subject = jnp.zeros((tok_blk,), jnp.int32)
    for which in range(SUBJ):
        subject = subject + jnp.where(region_ids == which + 1, region_identity[which], 0)
    key_subject = jnp.arange(SUBJ * IDTOK, dtype=jnp.int32) // IDTOK
    match = ((key_subject[None, :] == subject[:, None]) & has_id[:, None]).astype(f32)
    idpart = id_attend(q_own, id_kv, match)

    idpart, acc = lax.optimization_barrier((idpart, acc))
    whole = [first] + [shard for held in steps for shard in held]
    sums, lr = attend(text_count, queries, steps[-1], acc, everything=whole)

    pair = 2 * tok_blk
    recv = lax.ppermute(sums[pair:], "c", SWAP)
    lr_near, lr_send = lr[:, :, :pair], lr[:, :, pair:]
    lr_core = lax.ppermute(lr_send, "c", SWAP)
    lr_x = lax.ppermute(lr_near, "xl", SWAP)
    lr_far = lax.ppermute(lr_send, ("xl", "c"), [(i, 3 - i) for i in range(4)])
    mixed = combine(sums, recv, lr, lr_core, lr_x, lr_far, idpart)

    quarter = tok_blk // y_size
    mixed = mixed.reshape(2 * y_size, quarter, here)
    mixed = lax.all_to_all(mixed, ("xl", "y"), 0, 0, tiled=True)
    mine, other = project(mixed, [out_weight, before, after, far_low, far_high])
    return (mine + lax.ppermute(other, "xh", SWAP).astype(f32)).astype(bf16)


def solution(mesh):
    fine = Mesh(mesh.devices.reshape(2, 8, 2, 4, 2), BLK + ULY)
    placed = (
        P(BLK + ULY, None, None),
        P(),
        P(BLK),
        P(),
        P(None, BLK, None),
        P(None, BLK),
        P(),
        P(),
        P(None, None, ULY),
        P(ULY, None),
    )
    return jax.shard_map(
        on_device, mesh=fine, in_specs=placed, out_specs=P(BLK + ULY, None), check_vma=False
    )
```

```python
import functools
import math

import jax
import jax.numpy as jnp
from jax import lax
from jax.experimental import pallas as pl
from jax.experimental.pallas import tpu as pltpu
from jax.sharding import Mesh
from jax.sharding import PartitionSpec as P

HEAD = 128
TXT = 512
SUBJ = 4
IDTOK = 32
SCALE2 = math.log2(math.e) / math.sqrt(HEAD)
QT = 2048
SUB = 256
bf16 = jnp.bfloat16
f32 = jnp.float32
TRANSPOSED = (((1,), (1,)), ((), ()))
BLK = ("xl", "z", "c")
ULY = ("y", "xh")
SWAP = [(0, 1), (1, 0)]


def usable(count, mark):
    z, offset, size = mark
    text = (lax.axis_index("xl") == 0) & (lax.axis_index("c") == 0) & (lax.axis_index("z") == z)
    return jnp.where(text, jnp.clip(count - offset, 0, size), size)


def attn_kernel(marks, marks_all, first, last, sub, *refs):
    refs = list(refs)
    count = len(marks)
    text_count, q_ref = refs.pop(0), refs.pop(0)
    k_refs = [refs.pop(0) for _ in range(count)]
    v_refs = [refs.pop(0) for _ in range(count)]
    acc_in = None if first else refs.pop(0)
    if last:
        *shards, keep_ref, send_ref, lr_keep, lr_send, ones, acc_ref, k_buf, v_buf, top_ref = refs
    else:
        acc_ref, ones = refs
    head = pl.program_id(0)
    rows_here = q_ref.shape[0]
    keys = [r.shape[0] for r in k_refs]

    @pl.when((head == 0) & (pl.program_id(1) == 0))
    def _():
        at = 0
        for i in range(count):
            rows = lax.broadcasted_iota(jnp.int32, (keys[i], HEAD), 0)
            ones[at : at + keys[i], :] = jnp.where(rows < usable(text_count[0], marks[i]), 1.0, 0.0).astype(bf16)
            at += keys[i]

    def split(q):
        q = q.astype(f32) * SCALE2
        high = q.astype(bf16)
        return jnp.concatenate([high, (q - high.astype(f32)).astype(bf16)], axis=1)

    def score(q, k):
        return lax.dot_general(q, jnp.concatenate([k, k], axis=1), TRANSPOSED, preferred_element_type=f32)

    for start in range(0, rows_here, sub):
        total = None if first else acc_in[start : start + sub, :]
        q = split(q_ref[start : start + sub, :])
        at = 0
        for i in range(count):
            p = jnp.exp2(score(q, k_refs[i][...])).astype(bf16)
            v = jnp.concatenate([v_refs[i][...], ones[at : at + keys[i], :]], axis=1)
            part = jnp.dot(p, v, preferred_element_type=f32)
            total = part if total is None else total + part
            at += keys[i]
        acc_ref[start : start + sub, :] = total

    if last:
        half = rows_here // 2

        def write(totals, references):
            keep_ref[...] = acc_ref[:half, 0:HEAD].astype(bf16)
            send_ref[...] = acc_ref[half:, 0:HEAD].astype(bf16)
            for ref, part in ((lr_keep, slice(0, half)), (lr_send, slice(half, 2 * half))):
                ref[0:1, :] = totals[:, part]
                ref[1:2, :] = references[:, part]

        totals = acc_ref[:, HEAD : 2 * HEAD].T[0:1, :]
        write(totals, jnp.zeros_like(totals))
        good = jnp.min(jnp.where((totals >= 2.0**-60) & (totals <= 2.0**100), 1.0, 0.0)) > 0.5

        @pl.when(jnp.logical_not(good))
        def _():
            acc_ref[...] = jnp.zeros_like(acc_ref)
            top_ref[...] = jnp.full_like(top_ref, -1e30)
            for i, shard in enumerate(shards):
                here = slice(0, shard.shape[0])
                key_at = pl.multiple_of(head * HEAD, HEAD)
                value_at = pl.multiple_of(shard.shape[1] // 2 + head * HEAD, HEAD)
                pltpu.sync_copy(shard.at[:, pl.ds(key_at, HEAD)], k_buf.at[here, :])
                pltpu.sync_copy(shard.at[:, pl.ds(value_at, HEAD)], v_buf.at[here, :])
                for start in range(0, rows_here, sub):
                    part = slice(start, start + sub)
                    scores = score(split(q_ref[part, :]), k_buf[here, :])
                    key = lax.broadcasted_iota(jnp.int32, scores.shape, 1)
                    scores = jnp.where(key < usable(text_count[0], marks_all[i]), scores, -1e30)
                    old = top_ref[part, 0:1]
                    new = jnp.maximum(old, jnp.max(scores, axis=1, keepdims=True))
                    p = jnp.exp2(scores - new).astype(bf16)
                    v = v_buf[here, :]
                    v = jnp.concatenate([v, jnp.ones_like(v)], axis=1)
                    added = jnp.dot(p, v, preferred_element_type=f32)
                    acc_ref[part, :] = acc_ref[part, :] * jnp.exp2(old - new) + added
                    top_ref[part, :] = jnp.broadcast_to(new, (sub, HEAD))
            write(acc_ref[:, HEAD : 2 * HEAD].T[0:1, :], top_ref[...].T[0:1, :])


def attend(text_count, q, shards, acc, everything=None, tile=QT, sub=SUB):
    shards, marks = [kv for kv, _ in shards], [mark for _, mark in shards]
    first, last = acc is None, everything is not None
    marks_all = None
    rows = q.shape[0]
    heads = q.shape[1] // HEAD
    smem = pl.BlockSpec(memory_space=pltpu.SMEM)
    acc_block = pl.BlockSpec((None, tile, 2 * HEAD), lambda h, t: (h, t, 0))
    in_specs = [smem, pl.BlockSpec((tile, HEAD), lambda h, t: (t, h))]
    args = [text_count, q]
    for shift in (0, heads):
        for kv in shards:
            in_specs.append(pl.BlockSpec((kv.shape[0], HEAD), lambda h, t, s=shift: (0, s + h)))
            args.append(kv)
    if not first:
        in_specs.append(acc_block)
        args.append(acc)
    total = sum(kv.shape[0] for kv in shards)
    scratch = [pltpu.VMEM((total, HEAD), bf16)]
    if last:
        in_specs += [pl.BlockSpec(memory_space=pl.ANY)] * len(everything)
        args += [kv for kv, _ in everything]
        marks_all = [mark for _, mark in everything]
        half = tile // 2
        out_specs = [pl.BlockSpec((half, HEAD), lambda h, t: (0, h))] * 2
        out_specs += [pl.BlockSpec((None, 2, half), lambda h, t: (h, 0, 0))] * 2
        out_shape = [jax.ShapeDtypeStruct((half, heads * HEAD), bf16)] * 2
        out_shape += [jax.ShapeDtypeStruct((heads, 2, half), f32)] * 2
        keys = everything[0][0].shape[0]
        scratch += [
            pltpu.VMEM((tile, 2 * HEAD), f32),
            pltpu.VMEM((keys, HEAD), bf16),
            pltpu.VMEM((keys, HEAD), bf16),
            pltpu.VMEM((tile, HEAD), f32),
        ]
    else:
        out_specs = acc_block
        out_shape = jax.ShapeDtypeStruct((heads, rows, 2 * HEAD), f32)
    return pl.pallas_call(
        functools.partial(attn_kernel, marks, marks_all, first, last, sub),
        grid=(heads, rows // tile),
        in_specs=in_specs,
        out_specs=out_specs,
        out_shape=out_shape,
        scratch_shapes=scratch,
        cost_estimate=pl.CostEstimate(
            flops=heads * rows * total * 2048,
            bytes_accessed=12 * 2**20,
            transcendentals=heads * rows * total,
        ),
        compiler_params=pltpu.CompilerParams(vmem_limit_bytes=60 * 2**20),
    )(*args)


def id_kernel(q_ref, kv_ref, match_ref, out_ref):
    width = q_ref.shape[1]
    match = match_ref[...]
    lacking = 1.0 - jnp.max(match, axis=1, keepdims=True)
    for h in range(width // HEAD):
        cols = slice(h * HEAD, (h + 1) * HEAD)
        scores = lax.dot_general(
            q_ref[:, cols], kv_ref[:, cols], TRANSPOSED, preferred_element_type=f32
        ) * (1.0 / math.sqrt(HEAD))
        scores = jnp.where(match > 0, scores, -1e30)
        peak = jnp.max(scores, axis=1, keepdims=True)
        expo = jnp.exp(scores - peak) * match
        totals = jnp.sum(expo, axis=1, keepdims=True) + lacking
        v = kv_ref[:, width + h * HEAD : width + (h + 1) * HEAD]
        out_ref[:, cols] = jnp.dot(expo.astype(bf16), v, preferred_element_type=f32) / totals


def id_attend(q, id_kv, match):
    return pl.pallas_call(
        id_kernel,
        out_shape=jax.ShapeDtypeStruct(q.shape, f32),
        compiler_params=pltpu.CompilerParams(vmem_limit_bytes=32 * 2**20),
    )(q, id_kv, match)


def combine_kernel(keep, recv, lr_own, lr_core, lr_x, lr_far, id_ref, out_ref):
    slot = pl.program_id(0)
    tokens, width = keep.shape
    place = lax.rem(lax.axis_index("xl") + slot, 2)
    for h in range(width // HEAD):
        refs = [r[h, 1:2, :] for r in (lr_own, lr_core, lr_x, lr_far)]
        sums = [r[h, 0:1, :] for r in (lr_own, lr_core, lr_x, lr_far)]
        top = functools.reduce(jnp.maximum, refs)
        weight = [jnp.exp2(r - top) for r in refs]
        total = sum(w * s for w, s in zip(weight, sums))

        def column(row):
            return jnp.broadcast_to(row, (HEAD, tokens)).T

        cols = slice(h * HEAD, (h + 1) * HEAD)
        value = keep[:, cols].astype(f32) * column(weight[0] / total)
        value = value + recv[:, cols].astype(f32) * column(weight[1] / total)
        value = value + jnp.where(slot == 0, id_ref[:, cols], 0.0)
        out_ref[place, :, cols] = value.astype(bf16)


def combine(keep, recv, lr_keep, lr_core, lr_x, lr_far, idpart):
    tokens, width = idpart.shape
    heads = width // HEAD
    data = pl.BlockSpec((tokens, width), lambda s: (s, 0))
    near = pl.BlockSpec((heads, 2, tokens), lambda s: (0, 0, s))
    cross = pl.BlockSpec((heads, 2, tokens), lambda s: (0, 0, 1 - s))
    return pl.pallas_call(
        combine_kernel,
        grid=(2,),
        in_specs=[data, data, near, near, cross, cross, pl.BlockSpec((tokens, width), lambda s: (0, 0))],
        out_specs=pl.BlockSpec((2, tokens, width), lambda s: (0, 0, 0)),
        out_shape=jax.ShapeDtypeStruct((2, tokens, width), bf16),
        compiler_params=pltpu.CompilerParams(vmem_limit_bytes=60 * 2**20),
    )(keep, recv, lr_keep, lr_core, lr_x, lr_far, idpart)


def normalize(summed, id_gain):
    mean_square = jnp.mean(summed * summed, axis=-1, keepdims=True)
    return (summed * lax.rsqrt(mean_square + 1e-06) * id_gain).astype(bf16)


def identity_rows(gathered, latents, id_gain, id_kv_weight):
    width = latents.shape[1]
    feats, mix = gathered[:, :width], gathered[:, width : width + IDTOK]
    pooled = lax.dot_general(mix, feats, (((0,), (0,)), ((), ())), preferred_element_type=f32)
    tokens = normalize(latents.astype(f32) + pooled, id_gain)
    keys = jnp.dot(tokens, id_kv_weight[:, 0], preferred_element_type=f32)
    values = jnp.dot(tokens, id_kv_weight[:, 1], preferred_element_type=f32)
    return jnp.concatenate([keys, values], axis=1).astype(bf16)


def project_kernel(mixed, own, after, far, before, mine, other, product):
    y, xh = lax.axis_index("y"), lax.axis_index("xh")
    groups = mixed.shape[0] // 2

    def group(k):
        at = lax.rem(y + k, groups)
        return (mixed[at].astype(f32) + mixed[groups + at].astype(f32)).astype(bf16)

    total = jnp.dot(group(0), own[...], preferred_element_type=f32)
    for k, weight in ((1, after), (2, far), (3, before)):
        total += jnp.dot(group(k), weight[...], preferred_element_type=f32)
    product[...] = total
    rows = mine.shape[0]
    mine[...] = product[pl.ds(pl.multiple_of(xh * rows, rows), rows), :]
    other[...] = product[pl.ds(pl.multiple_of((1 - xh) * rows, rows), rows), :].astype(bf16)


def project(mixed, weights, part, parts):
    tokens, width = mixed.shape[1] // 2, weights[0].shape[1] // parts
    tile = 512
    start = part * width // tile
    columns = [pl.BlockSpec((w.shape[0], tile), lambda n: (0, start + n)) for w in weights]
    out = pl.BlockSpec((tokens, tile), lambda n: (0, n))
    return pl.pallas_call(
        project_kernel,
        grid=(width // tile,),
        in_specs=[pl.BlockSpec(mixed.shape, lambda n: (0, 0, 0))] + columns,
        out_specs=[out, out],
        out_shape=[
            jax.ShapeDtypeStruct((tokens, width), f32),
            jax.ShapeDtypeStruct((tokens, width), bf16),
        ],
        scratch_shapes=[pltpu.VMEM((2 * tokens, tile), f32)],
        cost_estimate=pl.CostEstimate(flops=2 * 10**9, bytes_accessed=10 * 2**20, transcendentals=0),
        compiler_params=pltpu.CompilerParams(vmem_limit_bytes=60 * 2**20),
    )(mixed, *weights)


def on_device(
    joint_qkv,
    text_count,
    region_ids,
    region_identity,
    id_feats,
    resample_mix,
    latents,
    id_gain,
    id_kv_weight,
    out_weight,
):
    z_size = lax.axis_size("z")
    y_size = lax.axis_size("y")
    uly = y_size * lax.axis_size("xh")
    tok_dev = joint_qkv.shape[0]
    tok_blk = tok_dev * uly
    width = joint_qkv.shape[2]
    here = width // uly
    my_xl, my_z, my_c = lax.axis_index("xl"), lax.axis_index("z"), lax.axis_index("c")
    number = lax.axis_index(ULY)

    block = (my_xl * z_size + my_z) * 2 + my_c
    here_feats = id_feats.shape[1]
    mix_rows = jnp.pad(resample_mix.T, ((0, 0), (0, HEAD - IDTOK)))
    mix_rows = jnp.broadcast_to(mix_rows, (SUBJ, here_feats, HEAD))
    packed = jnp.concatenate([id_feats, mix_rows], axis=2)
    packed, joint_qkv = lax.optimization_barrier((packed, joint_qkv))
    packed = lax.all_to_all(packed, ("xl", "c"), 0, 0, tiled=True)
    gathered = lax.all_gather(packed, "z", axis=0).reshape(-1, width + HEAD)

    by_group = joint_qkv.reshape(tok_dev, 3, uly, here)
    position = block * tok_blk + number * tok_dev + jnp.arange(tok_dev, dtype=jnp.int32)
    used = (position >= TXT) | (position < text_count[0])
    values = jnp.where(used[:, None, None], by_group[:, 2], 0)
    sent = jnp.concatenate([by_group[:, 0], by_group[:, 1], values], axis=-1).transpose(1, 0, 2)
    got = lax.all_to_all(sent, ULY, 0, 0, tiled=True).reshape(tok_blk, 3 * here)
    q_own, kv = got[:, :here], got[:, here:]
    q_x = lax.ppermute(q_own, "xl", SWAP)
    q_pair = jnp.concatenate([q_own, q_x], axis=0)
    queries = jnp.concatenate([q_pair, lax.ppermute(q_pair, "c", SWAP)], axis=0)

    around = lax.axis_size("y")
    onward = [(i, (i + 1) % around) for i in range(around)]
    backward = [(i, (i - 1) % around) for i in range(around)]
    before = lax.ppermute(out_weight, "y", onward)
    after = lax.ppermute(out_weight, "y", backward)

    right = [(i, (i + 1) % z_size) for i in range(z_size)]
    left = [(i, (i - 1) % z_size) for i in range(z_size)]
    half = tok_blk // 2
    end = z_size // 2
    first = (kv, (0, 0, tok_blk))
    up, down, acc = kv, kv, None
    pending = [first]
    whole = []
    for step in range(1, end + 1):
        if step < end:
            up, down = lax.ppermute(up, "z", right), lax.ppermute(down, "z", left)
            arriving = [(up, (step, 0, tok_blk)), (down, (z_size - step, 0, tok_blk))]
        else:
            up, down = lax.ppermute(up[:half], "z", right), lax.ppermute(down[half:], "z", left)
            arriving = [(up, (end, 0, half)), (down, (end, half, half))]
        acc = attend(text_count, queries, pending, acc)
        if step == 2:
            gathered, before, acc = lax.optimization_barrier((gathered, before, acc))
            far = lax.ppermute(before, "y", onward)
        if 1 < step < end:
            up, down, acc = lax.optimization_barrier((up, down, acc))
            arriving = [(up, arriving[0][1]), (down, arriving[1][1])]
        whole += pending
        pending = arriving
    whole += pending
    id_rows = identity_rows(gathered, latents, id_gain, id_kv_weight)
    id_core = lax.ppermute(id_rows, "c", SWAP)
    id_pair = jnp.where(my_c == 0, jnp.stack([id_rows, id_core]), jnp.stack([id_core, id_rows]))
    id_x = lax.ppermute(id_pair, "xl", SWAP)
    id_kv = jnp.where(my_xl == 0, jnp.stack([id_pair, id_x]), jnp.stack([id_x, id_pair]))
    id_kv = id_kv.reshape(SUBJ * IDTOK, 2 * here)
    position = block * tok_blk + jnp.arange(tok_blk, dtype=jnp.int32)
    has_id = (region_ids > 0) & (position >= TXT)
    subject = jnp.zeros((tok_blk,), jnp.int32)
    for which in range(SUBJ):
        subject = subject + jnp.where(region_ids == which + 1, region_identity[which], 0)
    key_subject = jnp.arange(SUBJ * IDTOK, dtype=jnp.int32) // IDTOK
    match = ((key_subject[None, :] == subject[:, None]) & has_id[:, None]).astype(f32)
    idpart = id_attend(q_own, id_kv, match)

    idpart, acc = lax.optimization_barrier((idpart, acc))
    keep, send, lr_keep, lr_send = attend(text_count, queries, pending, acc, everything=whole)

    far, send = lax.optimization_barrier((far, send))
    recv = lax.ppermute(send, "c", SWAP)
    lr_core = lax.ppermute(lr_send, "c", SWAP)
    lr_x = lax.ppermute(lr_keep, "xl", SWAP)
    lr_far = lax.ppermute(lr_send, ("xl", "c"), [(i, 3 - i) for i in range(4)])
    mixed = combine(keep, recv, lr_keep, lr_core, lr_x, lr_far, idpart)

    quarter = tok_blk // y_size
    mixed = mixed.reshape(2 * y_size, quarter, here)
    mixed = lax.all_to_all(mixed, ("xl", "y"), 0, 0, tiled=True)
    out = []
    for part in range(2):
        mine, other = project(mixed, [out_weight, after, far, before], part, 2)
        out.append((mine + lax.ppermute(other, "xh", SWAP).astype(f32)).astype(bf16))
    return jnp.concatenate(out, axis=1)


def solution(mesh):
    fine = Mesh(mesh.devices.reshape(2, 8, 2, 4, 2), BLK + ULY)
    placed = (
        P(BLK + ULY, None, None),
        P(),
        P(BLK),
        P(),
        P(None, BLK, None),
        P(None, BLK),
        P(),
        P(),
        P(None, None, ULY),
        P(ULY, None),
    )
    return jax.shard_map(
        on_device, mesh=fine, in_specs=placed, out_specs=P(BLK + ULY, None), check_vma=False
    )
```

```python
import functools
import math

import jax
import jax.numpy as jnp
from jax import lax
from jax.experimental import pallas as pl
from jax.experimental.pallas import tpu as pltpu
from jax.sharding import Mesh
from jax.sharding import PartitionSpec as P

HEAD = 128
TXT = 512
SUBJ = 4
IDTOK = 32
SCALE2 = math.log2(math.e) / math.sqrt(HEAD)
SUB = 256
bf16 = jnp.bfloat16
f32 = jnp.float32
TRANSPOSED = (((1,), (1,)), ((), ()))
BLK = ("xl", "z", "c")
ULY = ("y", "xh")
SWAP = [(0, 1), (1, 0)]


def usable(count, mark):
    z, offset, size = mark
    text = (lax.axis_index("xl") == 0) & (lax.axis_index("c") == 0) & (lax.axis_index("z") == z)
    return jnp.where(text, jnp.clip(count - offset, 0, size), size)


def attn_kernel(pieces, marks, marks_all, first, last, sub, *refs):
    refs = list(refs)
    count = len(marks)
    text_count = refs.pop(0)
    q_refs = [refs.pop(0) for _ in range(pieces)]
    k_refs = [refs.pop(0) for _ in range(count)]
    v_refs = [refs.pop(0) for _ in range(count)]
    acc_in = None if first else refs.pop(0)
    if last:
        *shards, keep_ref, send_ref, lr_keep, lr_send, ones, acc_ref, k_buf, v_buf, top_ref = refs
    else:
        acc_ref, ones = refs
    head = pl.program_id(0)
    piece_rows = q_refs[0].shape[0]
    rows_here = pieces * piece_rows
    keys = [r.shape[0] for r in k_refs]

    @pl.when(head == 0)
    def _():
        at = 0
        for i in range(count):
            rows = lax.broadcasted_iota(jnp.int32, (keys[i], HEAD), 0)
            ones[at : at + keys[i], :] = jnp.where(rows < usable(text_count[0], marks[i]), 1.0, 0.0).astype(bf16)
            at += keys[i]

    def split(start):
        at = start % piece_rows
        q = q_refs[start // piece_rows][at : at + sub, :].astype(f32) * SCALE2
        high = q.astype(bf16)
        return jnp.concatenate([high, (q - high.astype(f32)).astype(bf16)], axis=1)

    def score(q, k):
        return lax.dot_general(q, jnp.concatenate([k, k], axis=1), TRANSPOSED, preferred_element_type=f32)

    for start in range(0, rows_here, sub):
        total = None if first else acc_in[start : start + sub, :]
        q = split(start)
        at = 0
        for i in range(count):
            p = jnp.exp2(score(q, k_refs[i][...])).astype(bf16)
            v = jnp.concatenate([v_refs[i][...], ones[at : at + keys[i], :]], axis=1)
            part = jnp.dot(p, v, preferred_element_type=f32)
            total = part if total is None else total + part
            at += keys[i]
        acc_ref[start : start + sub, :] = total

    if last:
        half = rows_here // 2

        def write(totals, references):
            keep_ref[...] = acc_ref[:half, 0:HEAD].astype(bf16)
            send_ref[...] = acc_ref[half:, 0:HEAD].astype(bf16)
            for ref, part in ((lr_keep, slice(0, half)), (lr_send, slice(half, 2 * half))):
                ref[0:1, :] = totals[:, part]
                ref[1:2, :] = references[:, part]

        totals = acc_ref[:, HEAD : 2 * HEAD].T[0:1, :]
        write(totals, jnp.zeros_like(totals))
        good = jnp.min(jnp.where((totals >= 2.0**-60) & (totals <= 2.0**100), 1.0, 0.0)) > 0.5

        @pl.when(jnp.logical_not(good))
        def _():
            acc_ref[...] = jnp.zeros_like(acc_ref)
            top_ref[...] = jnp.full_like(top_ref, -1e30)
            for i, shard in enumerate(shards):
                here = slice(0, shard.shape[0])
                key_at = pl.multiple_of(head * HEAD, HEAD)
                value_at = pl.multiple_of(shard.shape[1] // 2 + head * HEAD, HEAD)
                pltpu.sync_copy(shard.at[:, pl.ds(key_at, HEAD)], k_buf.at[here, :])
                pltpu.sync_copy(shard.at[:, pl.ds(value_at, HEAD)], v_buf.at[here, :])
                for start in range(0, rows_here, sub):
                    part = slice(start, start + sub)
                    scores = score(split(start), k_buf[here, :])
                    key = lax.broadcasted_iota(jnp.int32, scores.shape, 1)
                    scores = jnp.where(key < usable(text_count[0], marks_all[i]), scores, -1e30)
                    old = top_ref[part, 0:1]
                    new = jnp.maximum(old, jnp.max(scores, axis=1, keepdims=True))
                    p = jnp.exp2(scores - new).astype(bf16)
                    v = v_buf[here, :]
                    v = jnp.concatenate([v, jnp.ones_like(v)], axis=1)
                    added = jnp.dot(p, v, preferred_element_type=f32)
                    acc_ref[part, :] = acc_ref[part, :] * jnp.exp2(old - new) + added
                    top_ref[part, :] = jnp.broadcast_to(new, (sub, HEAD))
            write(acc_ref[:, HEAD : 2 * HEAD].T[0:1, :], top_ref[...].T[0:1, :])


def attend(text_count, queries, shards, acc, everything=None, sub=SUB):
    shards, marks = [kv for kv, _ in shards], [mark for _, mark in shards]
    first, last = acc is None, everything is not None
    marks_all = None
    pieces = len(queries)
    rows = pieces * queries[0].shape[0]
    heads = queries[0].shape[1] // HEAD
    acc_block = pl.BlockSpec((None, rows, 2 * HEAD), lambda h: (h, 0, 0))
    in_specs = [pl.BlockSpec(memory_space=pltpu.SMEM)]
    in_specs += [pl.BlockSpec((q.shape[0], HEAD), lambda h: (0, h)) for q in queries]
    args = [text_count] + list(queries)
    for shift in (0, heads):
        for kv in shards:
            in_specs.append(pl.BlockSpec((kv.shape[0], HEAD), lambda h, s=shift: (0, s + h)))
            args.append(kv)
    if not first:
        in_specs.append(acc_block)
        args.append(acc)
    total = sum(kv.shape[0] for kv in shards)
    scratch = [pltpu.VMEM((total, HEAD), bf16)]
    if last:
        in_specs += [pl.BlockSpec(memory_space=pl.ANY)] * len(everything)
        args += [kv for kv, _ in everything]
        marks_all = [mark for _, mark in everything]
        half = rows // 2
        out_specs = [pl.BlockSpec((half, HEAD), lambda h: (0, h))] * 2
        out_specs += [pl.BlockSpec((None, 2, half), lambda h: (h, 0, 0))] * 2
        out_shape = [jax.ShapeDtypeStruct((half, heads * HEAD), bf16)] * 2
        out_shape += [jax.ShapeDtypeStruct((heads, 2, half), f32)] * 2
        keys = everything[0][0].shape[0]
        scratch += [
            pltpu.VMEM((rows, 2 * HEAD), f32),
            pltpu.VMEM((keys, HEAD), bf16),
            pltpu.VMEM((keys, HEAD), bf16),
            pltpu.VMEM((rows, HEAD), f32),
        ]
    else:
        out_specs = acc_block
        out_shape = jax.ShapeDtypeStruct((heads, rows, 2 * HEAD), f32)
    return pl.pallas_call(
        functools.partial(attn_kernel, pieces, marks, marks_all, first, last, sub),
        grid=(heads,),
        in_specs=in_specs,
        out_specs=out_specs,
        out_shape=out_shape,
        scratch_shapes=scratch,
        cost_estimate=pl.CostEstimate(
            flops=heads * rows * total * (1 if first else 2048),
            bytes_accessed=(1 if first else 12) * 2**20,
            transcendentals=0 if first else heads * rows * total,
        ),
        compiler_params=pltpu.CompilerParams(vmem_limit_bytes=60 * 2**20),
    )(*args)


def id_kernel(q_ref, kv_ref, match_ref, out_ref):
    width = q_ref.shape[1]
    match = match_ref[...]
    lacking = 1.0 - jnp.max(match, axis=1, keepdims=True)
    for h in range(width // HEAD):
        cols = slice(h * HEAD, (h + 1) * HEAD)
        scores = lax.dot_general(
            q_ref[:, cols], kv_ref[:, cols], TRANSPOSED, preferred_element_type=f32
        ) * (1.0 / math.sqrt(HEAD))
        scores = jnp.where(match > 0, scores, -1e30)
        peak = jnp.max(scores, axis=1, keepdims=True)
        expo = jnp.exp(scores - peak) * match
        totals = jnp.sum(expo, axis=1, keepdims=True) + lacking
        v = kv_ref[:, width + h * HEAD : width + (h + 1) * HEAD]
        out_ref[:, cols] = jnp.dot(expo.astype(bf16), v, preferred_element_type=f32) / totals


def id_attend(q, id_kv, match):
    return pl.pallas_call(
        id_kernel,
        out_shape=jax.ShapeDtypeStruct(q.shape, f32),
        compiler_params=pltpu.CompilerParams(vmem_limit_bytes=32 * 2**20),
    )(q, id_kv, match)


def combine_kernel(keep, recv, lr_own, lr_core, lr_x, lr_far, id_ref, out_ref):
    slot = pl.program_id(0)
    tokens, width = keep.shape
    place = lax.rem(lax.axis_index("xl") + slot, 2)
    for h in range(width // HEAD):
        refs = [r[h, 1:2, :] for r in (lr_own, lr_core, lr_x, lr_far)]
        sums = [r[h, 0:1, :] for r in (lr_own, lr_core, lr_x, lr_far)]
        top = functools.reduce(jnp.maximum, refs)
        weight = [jnp.exp2(r - top) for r in refs]
        total = sum(w * s for w, s in zip(weight, sums))

        def column(row):
            return jnp.broadcast_to(row, (HEAD, tokens)).T

        cols = slice(h * HEAD, (h + 1) * HEAD)
        value = keep[:, cols].astype(f32) * column(weight[0] / total)
        value = value + recv[:, cols].astype(f32) * column(weight[1] / total)
        value = value + jnp.where(slot == 0, id_ref[:, cols], 0.0)
        out_ref[place, :, cols] = value.astype(bf16)


def combine(keep, recv, lr_keep, lr_core, lr_x, lr_far, idpart):
    tokens, width = idpart.shape
    heads = width // HEAD
    data = pl.BlockSpec((tokens, width), lambda s: (s, 0))
    near = pl.BlockSpec((heads, 2, tokens), lambda s: (0, 0, s))
    cross = pl.BlockSpec((heads, 2, tokens), lambda s: (0, 0, 1 - s))
    return pl.pallas_call(
        combine_kernel,
        grid=(2,),
        in_specs=[data, data, near, near, cross, cross, pl.BlockSpec((tokens, width), lambda s: (0, 0))],
        out_specs=pl.BlockSpec((2, tokens, width), lambda s: (0, 0, 0)),
        out_shape=jax.ShapeDtypeStruct((2, tokens, width), bf16),
        compiler_params=pltpu.CompilerParams(vmem_limit_bytes=60 * 2**20),
    )(keep, recv, lr_keep, lr_core, lr_x, lr_far, idpart)


def normalize(summed, id_gain):
    mean_square = jnp.mean(summed * summed, axis=-1, keepdims=True)
    return (summed * lax.rsqrt(mean_square + 1e-06) * id_gain).astype(bf16)


def pooled_terms(gathered, width):
    return lax.dot_general(
        gathered[:, width:], gathered[:, :width], (((0,), (0,)), ((), ())), preferred_element_type=f32
    )


def identity_rows(pooled, latents, id_gain, id_kv_weight):
    tokens = normalize(latents.astype(f32) + pooled, id_gain)
    return jnp.dot(tokens, id_kv_weight, preferred_element_type=f32).astype(bf16)


def project_kernel(mixed, weight, mine, other, product):
    xh = lax.axis_index("xh")
    groups = weight.shape[0]
    total = None
    for y in range(groups):
        group = (mixed[y].astype(f32) + mixed[groups + y].astype(f32)).astype(bf16)
        part = jnp.dot(group, weight[y], preferred_element_type=f32)
        total = part if total is None else total + part
    product[...] = total
    rows = mine.shape[0]
    mine[...] = product[pl.ds(pl.multiple_of(xh * rows, rows), rows), :]
    other[...] = product[pl.ds(pl.multiple_of((1 - xh) * rows, rows), rows), :].astype(bf16)


def project(mixed, weight, part, parts):
    tokens, width = mixed.shape[1] // 2, weight.shape[2] // parts
    tile = 512
    start = part * width // tile
    columns = pl.BlockSpec(weight.shape[:2] + (tile,), lambda n: (0, 0, start + n))
    out = pl.BlockSpec((tokens, tile), lambda n: (0, n))
    return pl.pallas_call(
        project_kernel,
        grid=(width // tile,),
        in_specs=[pl.BlockSpec(mixed.shape, lambda n: (0, 0, 0)), columns],
        out_specs=[out, out],
        out_shape=[
            jax.ShapeDtypeStruct((tokens, width), f32),
            jax.ShapeDtypeStruct((tokens, width), bf16),
        ],
        scratch_shapes=[pltpu.VMEM((2 * tokens, tile), f32)],
        cost_estimate=pl.CostEstimate(flops=2 * 10**9, bytes_accessed=10 * 2**20, transcendentals=0),
        compiler_params=pltpu.CompilerParams(vmem_limit_bytes=16 * 2**20),
    )(mixed, weight)


def on_device(
    joint_qkv,
    text_count,
    region_ids,
    region_identity,
    id_feats,
    resample_mix,
    latents,
    id_gain,
    id_kv_weight,
    out_weight,
):
    z_size = lax.axis_size("z")
    y_size = lax.axis_size("y")
    uly = y_size * lax.axis_size("xh")
    tok_dev = joint_qkv.shape[0]
    tok_blk = tok_dev * uly
    width = joint_qkv.shape[2]
    here = width // uly
    my_xl, my_z, my_c = lax.axis_index("xl"), lax.axis_index("z"), lax.axis_index("c")
    number = lax.axis_index(ULY)

    block = (my_xl * z_size + my_z) * 2 + my_c
    lanes = jnp.arange(SUBJ * IDTOK, dtype=jnp.int32) // IDTOK
    own_lanes = lanes[None, None, :] == jnp.arange(SUBJ, dtype=jnp.int32)[:, None, None]
    mix_rows = jnp.where(own_lanes, jnp.tile(resample_mix.T, (1, SUBJ))[None], 0)
    packed = jnp.concatenate([id_feats, mix_rows], axis=2)
    gathered = lax.all_gather(packed, "z", axis=0).reshape(-1, width + SUBJ * IDTOK)

    by_group = joint_qkv.reshape(tok_dev, 3, uly, here)
    position = block * tok_blk + number * tok_dev + jnp.arange(tok_dev, dtype=jnp.int32)
    used = (position >= TXT) | (position < text_count[0])
    values = jnp.where(used[:, None, None], by_group[:, 2], 0)
    sent = jnp.concatenate([by_group[:, 0], by_group[:, 1], values], axis=-1).transpose(1, 0, 2)
    got = lax.all_to_all(sent, ULY, 0, 0, tiled=True).reshape(tok_blk, 3 * here)

    position = block * tok_blk + jnp.arange(tok_blk, dtype=jnp.int32)
    has_id = (region_ids > 0) & (position >= TXT)
    subject = jnp.zeros((tok_blk,), jnp.int32)
    for which in range(SUBJ):
        subject = subject + jnp.where(region_ids == which + 1, region_identity[which], 0)
    key_subject = jnp.arange(SUBJ * IDTOK, dtype=jnp.int32) // IDTOK
    match = ((key_subject[None, :] == subject[:, None]) & has_id[:, None]).astype(f32)
    flat_weight = id_kv_weight.reshape(width, 2 * here)
    got, match, flat_weight, out_weight = lax.optimization_barrier((got, match, flat_weight, out_weight))
    weight = lax.all_gather(out_weight, "y", axis=0)
    q_own, kv = lax.optimization_barrier((got[:, :here], got[:, here:]))
    q_x = lax.ppermute(q_own, "xl", SWAP)
    queries = [q_own, q_x, lax.ppermute(q_own, "c", SWAP), lax.ppermute(q_x, "c", SWAP)]

    right = [(i, (i + 1) % z_size) for i in range(z_size)]
    left = [(i, (i - 1) % z_size) for i in range(z_size)]
    half = tok_blk // 2
    end = z_size // 2
    first = (kv, (0, 0, tok_blk))
    up, down, acc = kv, kv, None
    pending = [first]
    whole = []
    for step in range(1, end + 1):
        if step < end:
            up, down = lax.ppermute(up, "z", right), lax.ppermute(down, "z", left)
            arriving = [(up, (step, 0, tok_blk)), (down, (z_size - step, 0, tok_blk))]
        else:
            up, down = lax.ppermute(up[:half], "z", right), lax.ppermute(down[half:], "z", left)
            arriving = [(up, (end, 0, half)), (down, (end, half, half))]
        acc = attend(text_count, queries, pending, acc)
        if step == 1:
            up, down, acc, gathered = lax.optimization_barrier((up, down, acc, gathered))
        elif step < end:
            up, down, acc = lax.optimization_barrier((up, down, acc))
        if step < end:
            arriving = [(up, arriving[0][1]), (down, arriving[1][1])]
        whole += pending
        pending = arriving
    whole += pending
    terms = pooled_terms(gathered, width).reshape(2, 2, IDTOK, width)
    terms = jnp.where(my_c == 0, terms[:, 0], terms[:, 1]) + lax.ppermute(
        jnp.where(my_c == 0, terms[:, 1], terms[:, 0]), "c", SWAP
    )
    pooled = jnp.where(my_xl == 0, terms[0], terms[1]) + lax.ppermute(
        jnp.where(my_xl == 0, terms[1], terms[0]), "xl", SWAP
    )
    id_rows = identity_rows(pooled, latents, id_gain, flat_weight)
    id_core = lax.ppermute(id_rows, "c", SWAP)
    id_pair = jnp.where(my_c == 0, jnp.stack([id_rows, id_core]), jnp.stack([id_core, id_rows]))
    id_x = lax.ppermute(id_pair, "xl", SWAP)
    id_kv = jnp.where(my_xl == 0, jnp.stack([id_pair, id_x]), jnp.stack([id_x, id_pair]))
    id_kv = id_kv.reshape(SUBJ * IDTOK, 2 * here)
    idpart = id_attend(q_own, id_kv, match)

    idpart, acc = lax.optimization_barrier((idpart, acc))
    keep, send, lr_keep, lr_send = attend(text_count, queries, pending, acc, everything=whole)

    recv = lax.ppermute(send, "c", SWAP)
    lr_core = lax.ppermute(lr_send, "c", SWAP)
    lr_x = lax.ppermute(lr_keep, "xl", SWAP)
    lr_far = lax.ppermute(lr_send, ("xl", "c"), [(i, 3 - i) for i in range(4)])
    mixed = combine(keep, recv, lr_keep, lr_core, lr_x, lr_far, idpart)

    quarter = tok_blk // y_size
    mixed = mixed.reshape(2 * y_size, quarter, here)
    mixed = lax.all_to_all(mixed, ("xl", "y"), 0, 0, tiled=True)
    out = []
    for part in range(2):
        mine, other = project(mixed, weight, part, 2)
        out.append((mine + lax.ppermute(other, "xh", SWAP).astype(f32)).astype(bf16))
    return jnp.concatenate(out, axis=1)


def solution(mesh):
    fine = Mesh(mesh.devices.reshape(2, 8, 2, 4, 2), BLK + ULY)
    placed = (
        P(BLK + ULY, None, None),
        P(),
        P(BLK),
        P(),
        P(None, BLK, None),
        P(None, BLK),
        P(),
        P(),
        P(None, None, ULY),
        P(ULY, None),
    )
    return jax.shard_map(
        on_device, mesh=fine, in_specs=placed, out_specs=P(BLK + ULY, None), check_vma=False
    )
```

```python
import functools
import math

import jax
import jax.numpy as jnp
from jax import lax
from jax.experimental import pallas as pl
from jax.experimental.pallas import tpu as pltpu
from jax.sharding import Mesh
from jax.sharding import PartitionSpec as P

HEAD = 128
TXT = 512
SUBJ = 4
IDTOK = 32
SCALE2 = math.log2(math.e) / math.sqrt(HEAD)
SUB = 256
bf16 = jnp.bfloat16
f32 = jnp.float32
TRANSPOSED = (((1,), (1,)), ((), ()))
BLK = ("xl", "z", "c")
ULY = ("y", "xh")
SWAP = [(0, 1), (1, 0)]


def usable(count, mark):
    z, offset, size = mark
    text = (lax.axis_index("xl") == 0) & (lax.axis_index("c") == 0) & (lax.axis_index("z") == z)
    return jnp.where(text, jnp.clip(count - offset, 0, size), size)


def attn_kernel(pieces, marks, marks_all, first, last, sub, *refs):
    refs = list(refs)
    count = len(marks)
    text_count = refs.pop(0)
    q_refs = [refs.pop(0) for _ in range(pieces)]
    k_refs = [refs.pop(0) for _ in range(count)]
    v_refs = [refs.pop(0) for _ in range(count)]
    acc_in = None if first else refs.pop(0)
    if last:
        *shards, keep_ref, send_ref, lr_keep, lr_send, ones, acc_ref, k_buf, v_buf, top_ref, q_buf = refs
    else:
        acc_ref, ones = refs
    head = pl.program_id(0)
    piece_rows = q_refs[0].shape[0]
    rows_here = pieces * piece_rows
    keys = [r.shape[0] for r in k_refs]

    @pl.when(head == 0)
    def _():
        at = 0
        for i in range(count):
            rows = lax.broadcasted_iota(jnp.int32, (keys[i], HEAD), 0)
            ones[at : at + keys[i], :] = jnp.where(rows < usable(text_count[0], marks[i]), 1.0, 0.0).astype(bf16)
            at += keys[i]

    def split(start):
        at = start % piece_rows
        q = q_refs[start // piece_rows][at : at + sub, :].astype(f32) * SCALE2
        high = q.astype(bf16)
        return jnp.concatenate([high, (q - high.astype(f32)).astype(bf16)], axis=1)

    def score(q, k):
        return lax.dot_general(q, jnp.concatenate([k, k], axis=1), TRANSPOSED, preferred_element_type=f32)

    for start in range(0, rows_here, sub):
        total = None if first else acc_in[start : start + sub, :]
        q = split(start)
        at = 0
        for i in range(count):
            p = jnp.exp2(score(q, k_refs[i][...])).astype(bf16)
            v = jnp.concatenate([v_refs[i][...], ones[at : at + keys[i], :]], axis=1)
            part = jnp.dot(p, v, preferred_element_type=f32)
            total = part if total is None else total + part
            at += keys[i]
        acc_ref[start : start + sub, :] = total

    if last:
        half = rows_here // 2

        def write(totals, references):
            keep_ref[...] = acc_ref[:half, 0:HEAD].astype(bf16)
            send_ref[...] = acc_ref[half:, 0:HEAD].astype(bf16)
            for ref, part in ((lr_keep, slice(0, half)), (lr_send, slice(half, 2 * half))):
                ref[0:1, :] = totals[:, part]
                ref[1:2, :] = references[:, part]

        def as_row(ref, first_lane):
            square = (HEAD, HEAD)
            diagonal = lax.broadcasted_iota(jnp.int32, square, 0) == lax.broadcasted_iota(jnp.int32, square, 1)
            parts = []
            for at in range(0, rows_here, HEAD):
                block = ref[at : at + HEAD, first_lane : first_lane + HEAD]
                parts.append(jnp.sum(jnp.where(diagonal, block, 0.0), axis=0, keepdims=True))
            return jnp.concatenate(parts, axis=1)

        totals = as_row(acc_ref, HEAD)
        write(totals, jnp.zeros_like(totals))
        good = jnp.min(jnp.where((totals >= 2.0**-60) & (totals <= 2.0**100), 1.0, 0.0)) > 0.5

        @pl.when(jnp.logical_not(good))
        def _():
            for start in range(0, rows_here, sub):
                q_buf[start : start + sub, :] = split(start)
            acc_ref[...] = jnp.zeros_like(acc_ref)
            top_ref[...] = jnp.full_like(top_ref, -1e30)
            for i, shard in enumerate(shards):
                here = slice(0, shard.shape[0])
                key_at = pl.multiple_of(head * HEAD, HEAD)
                value_at = pl.multiple_of(shard.shape[1] // 2 + head * HEAD, HEAD)
                pltpu.sync_copy(shard.at[:, pl.ds(key_at, HEAD)], k_buf.at[here, :])
                pltpu.sync_copy(shard.at[:, pl.ds(value_at, HEAD)], v_buf.at[here, :])
                limit = usable(text_count[0], marks_all[i])

                @pl.loop(0, rows_here // sub)
                def _(n):
                    part = pl.ds(pl.multiple_of(n * sub, sub), sub)
                    scores = score(q_buf[part, :], k_buf[here, :])
                    key = lax.broadcasted_iota(jnp.int32, scores.shape, 1)
                    scores = jnp.where(key < limit, scores, -1e30)
                    old = top_ref[part, :]
                    new = jnp.maximum(old, jnp.max(scores, axis=1, keepdims=True))
                    p = jnp.exp2(scores - new[:, 0:1]).astype(bf16)
                    v = v_buf[here, :]
                    v = jnp.concatenate([v, jnp.ones_like(v)], axis=1)
                    added = jnp.dot(p, v, preferred_element_type=f32)
                    factor = jnp.exp2(old - new)
                    acc_ref[part, :] = acc_ref[part, :] * jnp.concatenate([factor, factor], axis=1) + added
                    top_ref[part, :] = new

            write(as_row(acc_ref, HEAD), as_row(top_ref, 0))


def attend(text_count, queries, shards, acc, everything=None, sub=SUB):
    shards, marks = [kv for kv, _ in shards], [mark for _, mark in shards]
    first, last = acc is None, everything is not None
    marks_all = None
    pieces = len(queries)
    rows = pieces * queries[0].shape[0]
    heads = queries[0].shape[1] // HEAD
    acc_block = pl.BlockSpec((None, rows, 2 * HEAD), lambda h: (h, 0, 0))
    in_specs = [pl.BlockSpec(memory_space=pltpu.SMEM)]
    in_specs += [pl.BlockSpec((q.shape[0], HEAD), lambda h: (0, h)) for q in queries]
    args = [text_count] + list(queries)
    for shift in (0, heads):
        for kv in shards:
            in_specs.append(pl.BlockSpec((kv.shape[0], HEAD), lambda h, s=shift: (0, s + h)))
            args.append(kv)
    if not first:
        in_specs.append(acc_block)
        args.append(acc)
    total = sum(kv.shape[0] for kv in shards)
    scratch = [pltpu.VMEM((total, HEAD), bf16)]
    if last:
        in_specs += [pl.BlockSpec(memory_space=pl.ANY)] * len(everything)
        args += [kv for kv, _ in everything]
        marks_all = [mark for _, mark in everything]
        half = rows // 2
        out_specs = [pl.BlockSpec((half, HEAD), lambda h: (0, h))] * 2
        out_specs += [pl.BlockSpec((None, 2, half), lambda h: (h, 0, 0))] * 2
        out_shape = [jax.ShapeDtypeStruct((half, heads * HEAD), bf16)] * 2
        out_shape += [jax.ShapeDtypeStruct((heads, 2, half), f32)] * 2
        keys = everything[0][0].shape[0]
        scratch += [
            pltpu.VMEM((rows, 2 * HEAD), f32),
            pltpu.VMEM((keys, HEAD), bf16),
            pltpu.VMEM((keys, HEAD), bf16),
            pltpu.VMEM((rows, HEAD), f32),
            pltpu.VMEM((rows, 2 * HEAD), bf16),
        ]
    else:
        out_specs = acc_block
        out_shape = jax.ShapeDtypeStruct((heads, rows, 2 * HEAD), f32)
    return pl.pallas_call(
        functools.partial(attn_kernel, pieces, marks, marks_all, first, last, sub),
        grid=(heads,),
        in_specs=in_specs,
        out_specs=out_specs,
        out_shape=out_shape,
        scratch_shapes=scratch,
        cost_estimate=pl.CostEstimate(
            flops=heads * rows * total * (1 if first else 2048),
            bytes_accessed=(1 if first else 12) * 2**20,
            transcendentals=0 if first else heads * rows * total,
        ),
        compiler_params=pltpu.CompilerParams(vmem_limit_bytes=60 * 2**20),
    )(*args)


def id_kernel(q_ref, kv_ref, match_ref, out_ref):
    width = q_ref.shape[1]
    match = match_ref[...]
    lacking = 1.0 - jnp.max(match, axis=1, keepdims=True)
    for h in range(width // HEAD):
        cols = slice(h * HEAD, (h + 1) * HEAD)
        scores = lax.dot_general(
            q_ref[:, cols], kv_ref[:, cols], TRANSPOSED, preferred_element_type=f32
        ) * (1.0 / math.sqrt(HEAD))
        scores = jnp.where(match > 0, scores, -1e30)
        peak = jnp.max(scores, axis=1, keepdims=True)
        expo = jnp.exp(scores - peak) * match
        totals = jnp.sum(expo, axis=1, keepdims=True) + lacking
        v = kv_ref[:, width + h * HEAD : width + (h + 1) * HEAD]
        out_ref[:, cols] = jnp.dot(expo.astype(bf16), v, preferred_element_type=f32) / totals


def id_attend(q, id_kv, match):
    return pl.pallas_call(
        id_kernel,
        out_shape=jax.ShapeDtypeStruct(q.shape, f32),
        compiler_params=pltpu.CompilerParams(vmem_limit_bytes=32 * 2**20),
    )(q, id_kv, match)


def combine_kernel(keep, recv, lr_own, lr_core, lr_x, lr_far, id_ref, out_ref):
    slot = pl.program_id(0)
    tokens, width = keep.shape
    place = lax.rem(lax.axis_index("xl") + slot, 2)
    square = (HEAD, HEAD)
    diagonal = lax.broadcasted_iota(jnp.int32, square, 0) == lax.broadcasted_iota(jnp.int32, square, 1)
    for h in range(width // HEAD):
        refs = [r[h, 1:2, :] for r in (lr_own, lr_core, lr_x, lr_far)]
        sums = [r[h, 0:1, :] for r in (lr_own, lr_core, lr_x, lr_far)]
        top = functools.reduce(jnp.maximum, refs)
        weight = [jnp.exp2(r - top) for r in refs]
        total = sum(w * s for w, s in zip(weight, sums))

        scales = [weight[0] / total, weight[1] / total]
        for at in range(0, tokens, HEAD):
            rows, cols = slice(at, at + HEAD), slice(h * HEAD, (h + 1) * HEAD)
            left, right = [], []
            for scale, data in zip(scales, (keep, recv)):
                exact = jnp.where(diagonal, scale[:, rows], 0.0)
                high = exact.astype(bf16)
                left += [high, (exact - high.astype(f32)).astype(bf16)]
                right += [data[rows, cols]] * 2
            value = jnp.dot(
                jnp.concatenate(left, axis=1), jnp.concatenate(right, axis=0), preferred_element_type=f32
            )
            value = value + jnp.where(slot == 0, id_ref[rows, cols], 0.0)
            out_ref[place, rows, cols] = value.astype(bf16)


def combine(keep, recv, lr_keep, lr_core, lr_x, lr_far, idpart):
    tokens, width = idpart.shape
    heads = width // HEAD
    data = pl.BlockSpec((tokens, width), lambda s: (s, 0))
    near = pl.BlockSpec((heads, 2, tokens), lambda s: (0, 0, s))
    cross = pl.BlockSpec((heads, 2, tokens), lambda s: (0, 0, 1 - s))
    return pl.pallas_call(
        combine_kernel,
        grid=(2,),
        in_specs=[data, data, near, near, cross, cross, pl.BlockSpec((tokens, width), lambda s: (0, 0))],
        out_specs=pl.BlockSpec((2, tokens, width), lambda s: (0, 0, 0)),
        out_shape=jax.ShapeDtypeStruct((2, tokens, width), bf16),
        compiler_params=pltpu.CompilerParams(vmem_limit_bytes=16 * 2**20),
    )(keep, recv, lr_keep, lr_core, lr_x, lr_far, idpart)


def normalize(summed, id_gain):
    mean_square = jnp.mean(summed * summed, axis=-1, keepdims=True)
    return (summed * lax.rsqrt(mean_square + 1e-06) * id_gain).astype(bf16)


def pooled_terms(gathered, width):
    return lax.dot_general(
        gathered[:, width:], gathered[:, :width], (((0,), (0,)), ((), ())), preferred_element_type=f32
    )


def identity_rows(pooled, latents, id_gain, id_kv_weight):
    tokens = normalize(latents.astype(f32) + pooled, id_gain)
    return jnp.dot(tokens, id_kv_weight, preferred_element_type=f32).astype(bf16)


def project_kernel(mixed, weight, mine, other, product):
    xh = lax.axis_index("xh")
    groups = weight.shape[0]
    total = None
    for y in range(groups):
        group = (mixed[y].astype(f32) + mixed[groups + y].astype(f32)).astype(bf16)
        part = jnp.dot(group, weight[y], preferred_element_type=f32)
        total = part if total is None else total + part
    product[...] = total
    rows = mine.shape[0]
    mine[...] = product[pl.ds(pl.multiple_of(xh * rows, rows), rows), :]
    other[...] = product[pl.ds(pl.multiple_of((1 - xh) * rows, rows), rows), :].astype(bf16)


def project(mixed, weight, part, parts):
    tokens, width = mixed.shape[1] // 2, weight.shape[2] // parts
    tile = 512
    start = part * width // tile
    columns = pl.BlockSpec(weight.shape[:2] + (tile,), lambda n: (0, 0, start + n))
    out = pl.BlockSpec((tokens, tile), lambda n: (0, n))
    return pl.pallas_call(
        project_kernel,
        grid=(width // tile,),
        in_specs=[pl.BlockSpec(mixed.shape, lambda n: (0, 0, 0)), columns],
        out_specs=[out, out],
        out_shape=[
            jax.ShapeDtypeStruct((tokens, width), f32),
            jax.ShapeDtypeStruct((tokens, width), bf16),
        ],
        scratch_shapes=[pltpu.VMEM((2 * tokens, tile), f32)],
        cost_estimate=pl.CostEstimate(flops=2 * 10**9, bytes_accessed=10 * 2**20, transcendentals=0),
        compiler_params=pltpu.CompilerParams(vmem_limit_bytes=16 * 2**20),
    )(mixed, weight)


def on_device(
    joint_qkv,
    text_count,
    region_ids,
    region_identity,
    id_feats,
    resample_mix,
    latents,
    id_gain,
    id_kv_weight,
    out_weight,
):
    z_size = lax.axis_size("z")
    y_size = lax.axis_size("y")
    uly = y_size * lax.axis_size("xh")
    tok_dev = joint_qkv.shape[0]
    tok_blk = tok_dev * uly
    width = joint_qkv.shape[2]
    here = width // uly
    my_xl, my_z, my_c = lax.axis_index("xl"), lax.axis_index("z"), lax.axis_index("c")
    number = lax.axis_index(ULY)

    block = (my_xl * z_size + my_z) * 2 + my_c
    lanes = jnp.arange(SUBJ * IDTOK, dtype=jnp.int32) // IDTOK
    own_lanes = lanes[None, None, :] == jnp.arange(SUBJ, dtype=jnp.int32)[:, None, None]
    mix_rows = jnp.where(own_lanes, jnp.tile(resample_mix.T, (1, SUBJ))[None], 0)
    packed = jnp.concatenate([id_feats, mix_rows], axis=2)
    gathered = lax.all_gather(packed, "z", axis=0).reshape(-1, width + SUBJ * IDTOK)

    by_group = joint_qkv.reshape(tok_dev, 3, uly, here)
    position = block * tok_blk + number * tok_dev + jnp.arange(tok_dev, dtype=jnp.int32)
    used = (position >= TXT) | (position < text_count[0])
    values = jnp.where(used[:, None, None], by_group[:, 2], 0)
    sent = jnp.concatenate([by_group[:, 0], by_group[:, 1], values], axis=-1).transpose(1, 0, 2)
    got = lax.all_to_all(sent, ULY, 0, 0, tiled=True).reshape(tok_blk, 3 * here)

    position = block * tok_blk + jnp.arange(tok_blk, dtype=jnp.int32)
    has_id = (region_ids > 0) & (position >= TXT)
    subject = jnp.zeros((tok_blk,), jnp.int32)
    for which in range(SUBJ):
        subject = subject + jnp.where(region_ids == which + 1, region_identity[which], 0)
    key_subject = jnp.arange(SUBJ * IDTOK, dtype=jnp.int32) // IDTOK
    match = ((key_subject[None, :] == subject[:, None]) & has_id[:, None]).astype(f32)
    flat_weight = id_kv_weight.reshape(width, 2 * here)
    got, match, flat_weight, out_weight = lax.optimization_barrier((got, match, flat_weight, out_weight))
    weight = lax.all_gather(out_weight, "y", axis=0)
    q_own, kv = lax.optimization_barrier((got[:, :here], got[:, here:]))
    q_x = lax.ppermute(q_own, "xl", SWAP)
    queries = [q_own, q_x, lax.ppermute(q_own, "c", SWAP), lax.ppermute(q_x, "c", SWAP)]

    right = [(i, (i + 1) % z_size) for i in range(z_size)]
    left = [(i, (i - 1) % z_size) for i in range(z_size)]
    half = tok_blk // 2
    end = z_size // 2
    first = (kv, (0, 0, tok_blk))
    up, down, acc = kv, kv, None
    pending = [first]
    whole = []
    for step in range(1, end + 1):
        if step < end:
            up, down = lax.ppermute(up, "z", right), lax.ppermute(down, "z", left)
            arriving = [(up, (step, 0, tok_blk)), (down, (z_size - step, 0, tok_blk))]
        else:
            up, down = lax.ppermute(up[:half], "z", right), lax.ppermute(down[half:], "z", left)
            arriving = [(up, (end, 0, half)), (down, (end, half, half))]
        acc = attend(text_count, queries, pending, acc)
        if step == 1:
            up, down, acc = lax.optimization_barrier((up, down, acc))
        elif step == 2:
            acc, gathered = lax.optimization_barrier((acc, gathered))
            terms = pooled_terms(gathered, width).reshape(2, 2, IDTOK, width)
            own = jnp.where(my_c == 0, terms[:, 0], terms[:, 1])
            other = jnp.where(my_c == 0, terms[:, 1], terms[:, 0])
            up, down, acc, own, other = lax.optimization_barrier((up, down, acc, own, other))
            terms = own + lax.ppermute(other, "c", SWAP)
            pooled = jnp.where(my_xl == 0, terms[0], terms[1])
            pooled = pooled + lax.ppermute(jnp.where(my_xl == 0, terms[1], terms[0]), "xl", SWAP)
        elif step == end - 1:
            id_rows = identity_rows(pooled, latents, id_gain, flat_weight)
            up, down, acc, id_rows = lax.optimization_barrier((up, down, acc, id_rows))
        if step < end:
            arriving = [(up, arriving[0][1]), (down, arriving[1][1])]
        whole += pending
        pending = arriving
    whole += pending
    id_core = lax.ppermute(id_rows, "c", SWAP)
    id_pair = jnp.where(my_c == 0, jnp.stack([id_rows, id_core]), jnp.stack([id_core, id_rows]))
    id_pair, acc = lax.optimization_barrier((id_pair, acc))
    id_x = lax.ppermute(id_pair, "xl", SWAP)
    id_kv = jnp.where(my_xl == 0, jnp.stack([id_pair, id_x]), jnp.stack([id_x, id_pair]))
    id_kv = id_kv.reshape(SUBJ * IDTOK, 2 * here)
    idpart = id_attend(q_own, id_kv, match)
    keep, send, lr_keep, lr_send = attend(text_count, queries, pending, acc, everything=whole)

    recv = lax.ppermute(send, "c", SWAP)
    lr_core = lax.ppermute(lr_send, "c", SWAP)
    lr_x = lax.ppermute(lr_keep, "xl", SWAP)
    lr_far = lax.ppermute(lr_send, ("xl", "c"), [(i, 3 - i) for i in range(4)])
    mixed = combine(keep, recv, lr_keep, lr_core, lr_x, lr_far, idpart)

    quarter = tok_blk // y_size
    mixed = mixed.reshape(2 * y_size, quarter, here)
    mixed = lax.all_to_all(mixed, ("xl", "y"), 0, 0, tiled=True)
    out = []
    for part in range(2):
        mine, other = project(mixed, weight, part, 2)
        out.append((mine + lax.ppermute(other, "xh", SWAP).astype(f32)).astype(bf16))
    return jnp.concatenate(out, axis=1)


def solution(mesh):
    fine = Mesh(mesh.devices.reshape(2, 8, 2, 4, 2), BLK + ULY)
    placed = (
        P(BLK + ULY, None, None),
        P(),
        P(BLK),
        P(),
        P(None, BLK, None),
        P(None, BLK),
        P(),
        P(),
        P(None, None, ULY),
        P(ULY, None),
    )
    return jax.shard_map(
        on_device, mesh=fine, in_specs=placed, out_specs=P(BLK + ULY, None), check_vma=False
    )
```

```python
import functools
import math

import jax
import jax.numpy as jnp
from jax import lax
from jax.experimental import pallas as pl
from jax.experimental.pallas import tpu as pltpu
from jax.sharding import Mesh
from jax.sharding import PartitionSpec as P

HEAD = 128
TXT = 512
SUBJ = 4
IDTOK = 32
SCALE2 = math.log2(math.e) / math.sqrt(HEAD)
SUB = 256
bf16 = jnp.bfloat16
f32 = jnp.float32
TRANSPOSED = (((1,), (1,)), ((), ()))
BLK = ("xl", "z", "c")
ULY = ("y", "xh")
SWAP = [(0, 1), (1, 0)]


def usable(count, mark):
    z, offset, size = mark
    text = (lax.axis_index("xl") == 0) & (lax.axis_index("c") == 0) & (lax.axis_index("z") == z)
    return jnp.where(text, jnp.clip(count - offset, 0, size), size)


def attn_kernel(pieces, marks, marks_all, first, last, sub, *refs):
    refs = list(refs)
    count = len(marks)
    text_count = refs.pop(0)
    q_refs = [refs.pop(0) for _ in range(pieces)]
    k_refs = [refs.pop(0) for _ in range(count)]
    v_refs = [refs.pop(0) for _ in range(count)]
    acc_in = None if first else refs.pop(0)
    if last:
        *shards, keep_ref, send_ref, lr_keep, lr_send, ones, acc_ref, k_buf, v_buf, top_ref, q_buf = refs
    else:
        acc_ref, ones = refs
    head = pl.program_id(0)
    piece_rows = q_refs[0].shape[0]
    rows_here = pieces * piece_rows
    keys = [r.shape[0] for r in k_refs]

    @pl.when(head == 0)
    def _():
        at = 0
        for i in range(count):
            rows = lax.broadcasted_iota(jnp.int32, (keys[i], HEAD), 0)
            ones[at : at + keys[i], :] = jnp.where(rows < usable(text_count[0], marks[i]), 1.0, 0.0).astype(bf16)
            at += keys[i]

    def split(start):
        at = start % piece_rows
        q = q_refs[start // piece_rows][at : at + sub, :].astype(f32) * SCALE2
        high = q.astype(bf16)
        return jnp.concatenate([high, (q - high.astype(f32)).astype(bf16)], axis=1)

    def score(q, k):
        return lax.dot_general(q, jnp.concatenate([k, k], axis=1), TRANSPOSED, preferred_element_type=f32)

    for start in range(0, rows_here, sub):
        total = None if first else acc_in[start : start + sub, :]
        q = split(start)
        at = 0
        for i in range(count):
            p = jnp.exp2(score(q, k_refs[i][...])).astype(bf16)
            v = jnp.concatenate([v_refs[i][...], ones[at : at + keys[i], :]], axis=1)
            part = jnp.dot(p, v, preferred_element_type=f32)
            total = part if total is None else total + part
            at += keys[i]
        acc_ref[start : start + sub, :] = total

    if last:
        half = rows_here // 2

        def write(totals, references):
            keep_ref[...] = acc_ref[:half, 0:HEAD].astype(bf16)
            send_ref[...] = acc_ref[half:, 0:HEAD].astype(bf16)
            for ref, part in ((lr_keep, slice(0, half)), (lr_send, slice(half, 2 * half))):
                ref[0:1, :] = totals[:, part]
                ref[1:2, :] = references[:, part]

        def as_row(ref, first_lane):
            square = (HEAD, HEAD)
            diagonal = lax.broadcasted_iota(jnp.int32, square, 0) == lax.broadcasted_iota(jnp.int32, square, 1)
            parts = []
            for at in range(0, rows_here, HEAD):
                block = ref[at : at + HEAD, first_lane : first_lane + HEAD]
                parts.append(jnp.sum(jnp.where(diagonal, block, 0.0), axis=0, keepdims=True))
            return jnp.concatenate(parts, axis=1)

        totals = as_row(acc_ref, HEAD)
        write(totals, jnp.zeros_like(totals))
        good = jnp.min(jnp.where((totals >= 2.0**-60) & (totals <= 2.0**100), 1.0, 0.0)) > 0.5

        @pl.when(jnp.logical_not(good))
        def _():
            for start in range(0, rows_here, sub):
                q_buf[start : start + sub, :] = split(start)
            acc_ref[...] = jnp.zeros_like(acc_ref)
            top_ref[...] = jnp.full_like(top_ref, -1e30)
            for i, shard in enumerate(shards):
                here = slice(0, shard.shape[0])
                key_at = pl.multiple_of(head * HEAD, HEAD)
                value_at = pl.multiple_of(shard.shape[1] // 2 + head * HEAD, HEAD)
                pltpu.sync_copy(shard.at[:, pl.ds(key_at, HEAD)], k_buf.at[here, :])
                pltpu.sync_copy(shard.at[:, pl.ds(value_at, HEAD)], v_buf.at[here, :])
                limit = usable(text_count[0], marks_all[i])

                @pl.loop(0, rows_here // sub)
                def _(n):
                    part = pl.ds(pl.multiple_of(n * sub, sub), sub)
                    scores = score(q_buf[part, :], k_buf[here, :])
                    key = lax.broadcasted_iota(jnp.int32, scores.shape, 1)
                    scores = jnp.where(key < limit, scores, -1e30)
                    old = top_ref[part, :]
                    new = jnp.maximum(old, jnp.max(scores, axis=1, keepdims=True))
                    p = jnp.exp2(scores - new[:, 0:1]).astype(bf16)
                    v = v_buf[here, :]
                    v = jnp.concatenate([v, jnp.ones_like(v)], axis=1)
                    added = jnp.dot(p, v, preferred_element_type=f32)
                    factor = jnp.exp2(old - new)
                    acc_ref[part, :] = acc_ref[part, :] * jnp.concatenate([factor, factor], axis=1) + added
                    top_ref[part, :] = new

            write(as_row(acc_ref, HEAD), as_row(top_ref, 0))


def attend(text_count, queries, shards, acc, everything=None, sub=SUB):
    shards, marks = [kv for kv, _ in shards], [mark for _, mark in shards]
    first, last = acc is None, everything is not None
    marks_all = None
    pieces = len(queries)
    rows = pieces * queries[0].shape[0]
    heads = queries[0].shape[1] // HEAD
    acc_block = pl.BlockSpec((None, rows, 2 * HEAD), lambda h: (h, 0, 0))
    in_specs = [pl.BlockSpec(memory_space=pltpu.SMEM)]
    in_specs += [pl.BlockSpec((q.shape[0], HEAD), lambda h: (0, h)) for q in queries]
    args = [text_count] + list(queries)
    for shift in (0, heads):
        for kv in shards:
            in_specs.append(pl.BlockSpec((kv.shape[0], HEAD), lambda h, s=shift: (0, s + h)))
            args.append(kv)
    if not first:
        in_specs.append(acc_block)
        args.append(acc)
    total = sum(kv.shape[0] for kv in shards)
    scratch = [pltpu.VMEM((total, HEAD), bf16)]
    if last:
        in_specs += [pl.BlockSpec(memory_space=pl.ANY)] * len(everything)
        args += [kv for kv, _ in everything]
        marks_all = [mark for _, mark in everything]
        half = rows // 2
        out_specs = [pl.BlockSpec((half, HEAD), lambda h: (0, h))] * 2
        out_specs += [pl.BlockSpec((None, 2, half), lambda h: (h, 0, 0))] * 2
        out_shape = [jax.ShapeDtypeStruct((half, heads * HEAD), bf16)] * 2
        out_shape += [jax.ShapeDtypeStruct((heads, 2, half), f32)] * 2
        keys = everything[0][0].shape[0]
        scratch += [
            pltpu.VMEM((rows, 2 * HEAD), f32),
            pltpu.VMEM((keys, HEAD), bf16),
            pltpu.VMEM((keys, HEAD), bf16),
            pltpu.VMEM((rows, HEAD), f32),
            pltpu.VMEM((rows, 2 * HEAD), bf16),
        ]
    else:
        out_specs = acc_block
        out_shape = jax.ShapeDtypeStruct((heads, rows, 2 * HEAD), f32)
    return pl.pallas_call(
        functools.partial(attn_kernel, pieces, marks, marks_all, first, last, sub),
        grid=(heads,),
        in_specs=in_specs,
        out_specs=out_specs,
        out_shape=out_shape,
        scratch_shapes=scratch,
        cost_estimate=pl.CostEstimate(
            flops=heads * rows * total * (1 if first else 2048),
            bytes_accessed=(1 if first else 12) * 2**20,
            transcendentals=0 if first else heads * rows * total,
        ),
        compiler_params=pltpu.CompilerParams(vmem_limit_bytes=58 * 2**20),
    )(*args)


def id_kernel(q_ref, kv_ref, match_ref, out_ref):
    width = q_ref.shape[1]
    match = match_ref[...]
    lacking = 1.0 - jnp.max(match, axis=1, keepdims=True)
    for h in range(width // HEAD):
        cols = slice(h * HEAD, (h + 1) * HEAD)
        scores = lax.dot_general(
            q_ref[:, cols], kv_ref[:, cols], TRANSPOSED, preferred_element_type=f32
        ) * (1.0 / math.sqrt(HEAD))
        scores = jnp.where(match > 0, scores, -1e30)
        peak = jnp.max(scores, axis=1, keepdims=True)
        expo = jnp.exp(scores - peak) * match
        totals = jnp.sum(expo, axis=1, keepdims=True) + lacking
        v = kv_ref[:, width + h * HEAD : width + (h + 1) * HEAD]
        out_ref[:, cols] = jnp.dot(expo.astype(bf16), v, preferred_element_type=f32) / totals


def id_attend(q, id_kv, match):
    return pl.pallas_call(
        id_kernel,
        out_shape=jax.ShapeDtypeStruct(q.shape, f32),
        compiler_params=pltpu.CompilerParams(vmem_limit_bytes=32 * 2**20),
    )(q, id_kv, match)


def combine_kernel(keep, recv, lr_own, lr_core, lr_x, lr_far, id_ref, out_ref):
    slot = pl.program_id(0)
    tokens, width = keep.shape
    place = lax.rem(lax.axis_index("xl") + slot, 2)
    square = (HEAD, HEAD)
    diagonal = lax.broadcasted_iota(jnp.int32, square, 0) == lax.broadcasted_iota(jnp.int32, square, 1)
    for h in range(width // HEAD):
        refs = [r[h, 1:2, :] for r in (lr_own, lr_core, lr_x, lr_far)]
        sums = [r[h, 0:1, :] for r in (lr_own, lr_core, lr_x, lr_far)]
        top = functools.reduce(jnp.maximum, refs)
        weight = [jnp.exp2(r - top) for r in refs]
        total = sum(w * s for w, s in zip(weight, sums))

        scales = [weight[0] / total, weight[1] / total]
        for at in range(0, tokens, HEAD):
            rows, cols = slice(at, at + HEAD), slice(h * HEAD, (h + 1) * HEAD)
            left, right = [], []
            for scale, data in zip(scales, (keep, recv)):
                exact = jnp.where(diagonal, scale[:, rows], 0.0)
                high = exact.astype(bf16)
                left += [high, (exact - high.astype(f32)).astype(bf16)]
                right += [data[rows, cols]] * 2
            value = jnp.dot(
                jnp.concatenate(left, axis=1), jnp.concatenate(right, axis=0), preferred_element_type=f32
            )
            value = value + jnp.where(slot == 0, id_ref[rows, cols], 0.0)
            out_ref[place, rows, cols] = value.astype(bf16)


def combine(keep, recv, lr_keep, lr_core, lr_x, lr_far, idpart):
    tokens, width = idpart.shape
    heads = width // HEAD
    data = pl.BlockSpec((tokens, width), lambda s: (s, 0))
    near = pl.BlockSpec((heads, 2, tokens), lambda s: (0, 0, s))
    cross = pl.BlockSpec((heads, 2, tokens), lambda s: (0, 0, 1 - s))
    return pl.pallas_call(
        combine_kernel,
        grid=(2,),
        in_specs=[data, data, near, near, cross, cross, pl.BlockSpec((tokens, width), lambda s: (0, 0))],
        out_specs=pl.BlockSpec((2, tokens, width), lambda s: (0, 0, 0)),
        out_shape=jax.ShapeDtypeStruct((2, tokens, width), bf16),
        compiler_params=pltpu.CompilerParams(vmem_limit_bytes=16 * 2**20),
    )(keep, recv, lr_keep, lr_core, lr_x, lr_far, idpart)


def normalize(summed, id_gain):
    mean_square = jnp.mean(summed * summed, axis=-1, keepdims=True)
    return (summed * lax.rsqrt(mean_square + 1e-06) * id_gain).astype(bf16)


def pooled_terms(gathered, width):
    return lax.dot_general(
        gathered[:, width:], gathered[:, :width], (((0,), (0,)), ((), ())), preferred_element_type=f32
    )


def identity_rows(pooled, latents, id_gain, id_kv_weight):
    tokens = normalize(latents.astype(f32) + pooled, id_gain)
    return jnp.dot(tokens, id_kv_weight, preferred_element_type=f32).astype(bf16)


def project_kernel(mixed, weight, mine, other, product):
    xh = lax.axis_index("xh")
    groups = weight.shape[0]
    total = None
    for y in range(groups):
        group = (mixed[y].astype(f32) + mixed[groups + y].astype(f32)).astype(bf16)
        part = jnp.dot(group, weight[y], preferred_element_type=f32)
        total = part if total is None else total + part
    product[...] = total
    rows = mine.shape[0]
    mine[...] = product[pl.ds(pl.multiple_of(xh * rows, rows), rows), :]
    other[...] = product[pl.ds(pl.multiple_of((1 - xh) * rows, rows), rows), :].astype(bf16)


def project(mixed, weight):
    tokens, width = mixed.shape[1] // 2, weight.shape[2]
    tile = 512
    columns = pl.BlockSpec(weight.shape[:2] + (tile,), lambda n: (0, 0, n))
    out = pl.BlockSpec((tokens, tile), lambda n: (0, n))
    return pl.pallas_call(
        project_kernel,
        grid=(width // tile,),
        in_specs=[pl.BlockSpec(mixed.shape, lambda n: (0, 0, 0)), columns],
        out_specs=[out, out],
        out_shape=[
            jax.ShapeDtypeStruct((tokens, width), f32),
            jax.ShapeDtypeStruct((tokens, width), bf16),
        ],
        scratch_shapes=[pltpu.VMEM((2 * tokens, tile), f32)],
        cost_estimate=pl.CostEstimate(flops=2 * 10**9, bytes_accessed=10 * 2**20, transcendentals=0),
        compiler_params=pltpu.CompilerParams(vmem_limit_bytes=16 * 2**20),
    )(mixed, weight)


def on_device(
    joint_qkv,
    text_count,
    region_ids,
    region_identity,
    id_feats,
    resample_mix,
    latents,
    id_gain,
    id_kv_weight,
    out_weight,
):
    z_size = lax.axis_size("z")
    y_size = lax.axis_size("y")
    uly = y_size * lax.axis_size("xh")
    tok_dev = joint_qkv.shape[0]
    tok_blk = tok_dev * uly
    width = joint_qkv.shape[2]
    here = width // uly
    my_xl, my_z, my_c = lax.axis_index("xl"), lax.axis_index("z"), lax.axis_index("c")
    number = lax.axis_index(ULY)

    block = (my_xl * z_size + my_z) * 2 + my_c
    lanes = jnp.arange(SUBJ * IDTOK, dtype=jnp.int32) // IDTOK
    own_lanes = lanes[None, None, :] == jnp.arange(SUBJ, dtype=jnp.int32)[:, None, None]
    mix_rows = jnp.where(own_lanes, jnp.tile(resample_mix.T, (1, SUBJ))[None], 0)
    packed = jnp.concatenate([id_feats, mix_rows], axis=2)
    gathered = lax.all_gather(packed, "z", axis=0).reshape(-1, width + SUBJ * IDTOK)

    by_group = joint_qkv.reshape(tok_dev, 3, uly, here)
    position = block * tok_blk + number * tok_dev + jnp.arange(tok_dev, dtype=jnp.int32)
    used = (position >= TXT) | (position < text_count[0])
    values = jnp.where(used[:, None, None], by_group[:, 2], 0)
    sent = jnp.concatenate([by_group[:, 0], by_group[:, 1], values], axis=-1).transpose(1, 0, 2)
    got = lax.all_to_all(sent, ULY, 0, 0, tiled=True).reshape(tok_blk, 3 * here)

    position = block * tok_blk + jnp.arange(tok_blk, dtype=jnp.int32)
    has_id = (region_ids > 0) & (position >= TXT)
    subject = jnp.zeros((tok_blk,), jnp.int32)
    for which in range(SUBJ):
        subject = subject + jnp.where(region_ids == which + 1, region_identity[which], 0)
    key_subject = jnp.arange(SUBJ * IDTOK, dtype=jnp.int32) // IDTOK
    match = ((key_subject[None, :] == subject[:, None]) & has_id[:, None]).astype(f32)
    flat_weight = id_kv_weight.reshape(width, 2 * here)
    half_weight = jnp.where(my_c == 0, out_weight[:, : width // 2], out_weight[:, width // 2 :])
    got, match, flat_weight, half_weight = lax.optimization_barrier((got, match, flat_weight, half_weight))
    weight = lax.all_gather(half_weight, "y", axis=0)
    q_own, kv = lax.optimization_barrier((got[:, :here], got[:, here:]))
    q_x = lax.ppermute(q_own, "xl", SWAP)
    queries = [q_own, q_x, lax.ppermute(q_own, "c", SWAP), lax.ppermute(q_x, "c", SWAP)]

    right = [(i, (i + 1) % z_size) for i in range(z_size)]
    left = [(i, (i - 1) % z_size) for i in range(z_size)]
    half = tok_blk // 2
    end = z_size // 2
    first = (kv, (0, 0, tok_blk))
    up, down, acc = kv, kv, None
    pending = [first]
    whole = []
    for step in range(1, end + 1):
        if step < end:
            up, down = lax.ppermute(up, "z", right), lax.ppermute(down, "z", left)
            arriving = [(up, (step, 0, tok_blk)), (down, (z_size - step, 0, tok_blk))]
        else:
            up, down = lax.ppermute(up[:half], "z", right), lax.ppermute(down[half:], "z", left)
            arriving = [(up, (end, 0, half)), (down, (end, half, half))]
        acc = attend(text_count, queries, pending, acc)
        if step == 1:
            up, down, acc = lax.optimization_barrier((up, down, acc))
        elif step == 2:
            acc, gathered = lax.optimization_barrier((acc, gathered))
            terms = pooled_terms(gathered, width).reshape(2, 2, IDTOK, width)
            own = jnp.where(my_c == 0, terms[:, 0], terms[:, 1])
            other = jnp.where(my_c == 0, terms[:, 1], terms[:, 0])
            up, down, acc, own, other = lax.optimization_barrier((up, down, acc, own, other))
            terms = own + lax.ppermute(other, "c", SWAP)
            pooled = jnp.where(my_xl == 0, terms[0], terms[1])
            pooled = pooled + lax.ppermute(jnp.where(my_xl == 0, terms[1], terms[0]), "xl", SWAP)
        elif step == end - 1:
            id_rows = identity_rows(pooled, latents, id_gain, flat_weight)
            up, down, acc, id_rows = lax.optimization_barrier((up, down, acc, id_rows))
        if step < end:
            arriving = [(up, arriving[0][1]), (down, arriving[1][1])]
        whole += pending
        pending = arriving
    whole += pending
    id_core = lax.ppermute(id_rows, "c", SWAP)
    id_pair = jnp.where(my_c == 0, jnp.stack([id_rows, id_core]), jnp.stack([id_core, id_rows]))
    id_pair, acc = lax.optimization_barrier((id_pair, acc))
    id_x = lax.ppermute(id_pair, "xl", SWAP)
    id_kv = jnp.where(my_xl == 0, jnp.stack([id_pair, id_x]), jnp.stack([id_x, id_pair]))
    id_kv = id_kv.reshape(SUBJ * IDTOK, 2 * here)
    idpart = id_attend(q_own, id_kv, match)
    keep, send, lr_keep, lr_send = attend(text_count, queries, pending, acc, everything=whole)

    recv = lax.ppermute(send, "c", SWAP)
    lr_core = lax.ppermute(lr_send, "c", SWAP)
    lr_x = lax.ppermute(lr_keep, "xl", SWAP)
    lr_far = lax.ppermute(lr_send, ("xl", "c"), [(i, 3 - i) for i in range(4)])
    weight, recv, lr_core, lr_x, lr_far, idpart = lax.optimization_barrier(
        (weight, recv, lr_core, lr_x, lr_far, idpart)
    )
    other_weight = lax.ppermute(weight, "c", SWAP)
    mixed = combine(keep, recv, lr_keep, lr_core, lr_x, lr_far, idpart)

    quarter = tok_blk // y_size
    mixed = mixed.reshape(2 * y_size, quarter, here)
    weight, mixed = lax.optimization_barrier((weight, mixed))
    mixed = lax.all_to_all(mixed, ("xl", "y"), 0, 0, tiled=True)
    out = []
    for columns in (weight, other_weight):
        mine, other = project(mixed, columns)
        out.append((mine + lax.ppermute(other, "xh", SWAP).astype(f32)).astype(bf16))
    low = jnp.where(my_c == 0, out[0], out[1])
    high = jnp.where(my_c == 0, out[1], out[0])
    return jnp.concatenate([low, high], axis=1)


def solution(mesh):
    fine = Mesh(mesh.devices.reshape(2, 8, 2, 4, 2), BLK + ULY)
    placed = (
        P(BLK + ULY, None, None),
        P(),
        P(BLK),
        P(),
        P(None, BLK, None),
        P(None, BLK),
        P(),
        P(),
        P(None, None, ULY),
        P(ULY, None),
    )
    return jax.shard_map(
        on_device, mesh=fine, in_specs=placed, out_specs=P(BLK + ULY, None), check_vma=False
    )
```

```python
import functools
import math

import jax
import jax.numpy as jnp
from jax import lax
from jax.experimental import pallas as pl
from jax.experimental.pallas import tpu as pltpu
from jax.sharding import Mesh
from jax.sharding import PartitionSpec as P

HEAD = 128
TXT = 512
SUBJ = 4
IDTOK = 32
SCALE2 = math.log2(math.e) / math.sqrt(HEAD)
SUB = 256
bf16 = jnp.bfloat16
f32 = jnp.float32
TRANSPOSED = (((1,), (1,)), ((), ()))
BLK = ("xl", "z", "c")
ULY = ("y", "xh")
SWAP = [(0, 1), (1, 0)]


def usable(count, mark):
    z, offset, size = mark
    text = (lax.axis_index("xl") == 0) & (lax.axis_index("c") == 0) & (lax.axis_index("z") == z)
    return jnp.where(text, jnp.clip(count - offset, 0, size), size)


def attn_kernel(pieces, marks, marks_all, first, last, sub, *refs):
    refs = list(refs)
    count = len(marks)
    text_count = refs.pop(0)
    q_refs = [refs.pop(0) for _ in range(pieces)]
    k_refs = [refs.pop(0) for _ in range(count)]
    v_refs = [refs.pop(0) for _ in range(count)]
    acc_in = None if first else refs.pop(0)
    if last:
        *shards, keep_ref, send_ref, lr_keep, lr_send, ones, acc_ref, k_buf, v_buf, top_ref, q_buf = refs
    else:
        acc_ref, ones = refs
    head = pl.program_id(0)
    piece_rows = q_refs[0].shape[0]
    rows_here = pieces * piece_rows
    keys = [r.shape[0] for r in k_refs]

    @pl.when(head == 0)
    def _():
        at = 0
        for i in range(count):
            rows = lax.broadcasted_iota(jnp.int32, (keys[i], HEAD), 0)
            ones[at : at + keys[i], :] = jnp.where(rows < usable(text_count[0], marks[i]), 1.0, 0.0).astype(bf16)
            at += keys[i]

    def split(start):
        at = start % piece_rows
        q = q_refs[start // piece_rows][at : at + sub, :].astype(f32) * SCALE2
        high = q.astype(bf16)
        return jnp.concatenate([high, (q - high.astype(f32)).astype(bf16)], axis=1)

    def score(q, k):
        return lax.dot_general(q, jnp.concatenate([k, k], axis=1), TRANSPOSED, preferred_element_type=f32)

    for start in range(0, rows_here, sub):
        total = None if first else acc_in[start : start + sub, :]
        q = split(start)
        at = 0
        for i in range(count):
            p = jnp.exp2(score(q, k_refs[i][...])).astype(bf16)
            v = jnp.concatenate([v_refs[i][...], ones[at : at + keys[i], :]], axis=1)
            part = jnp.dot(p, v, preferred_element_type=f32)
            total = part if total is None else total + part
            at += keys[i]
        acc_ref[start : start + sub, :] = total

    if last:
        half = rows_here // 2

        def write(totals, references):
            keep_ref[...] = acc_ref[:half, 0:HEAD].astype(bf16)
            send_ref[...] = acc_ref[half:, 0:HEAD].astype(bf16)
            for ref, part in ((lr_keep, slice(0, half)), (lr_send, slice(half, 2 * half))):
                ref[0:1, :] = totals[:, part]
                ref[1:2, :] = references[:, part]

        def as_row(ref, first_lane):
            square = (HEAD, HEAD)
            diagonal = lax.broadcasted_iota(jnp.int32, square, 0) == lax.broadcasted_iota(jnp.int32, square, 1)
            parts = []
            for at in range(0, rows_here, HEAD):
                block = ref[at : at + HEAD, first_lane : first_lane + HEAD]
                parts.append(jnp.sum(jnp.where(diagonal, block, 0.0), axis=0, keepdims=True))
            return jnp.concatenate(parts, axis=1)

        totals = as_row(acc_ref, HEAD)
        write(totals, jnp.zeros_like(totals))
        good = jnp.min(jnp.where((totals >= 2.0**-60) & (totals <= 2.0**100), 1.0, 0.0)) > 0.5

        @pl.when(jnp.logical_not(good))
        def _():
            for start in range(0, rows_here, sub):
                q_buf[start : start + sub, :] = split(start)
            acc_ref[...] = jnp.zeros_like(acc_ref)
            top_ref[...] = jnp.full_like(top_ref, -1e30)
            for i, shard in enumerate(shards):
                here = slice(0, shard.shape[0])
                key_at = pl.multiple_of(head * HEAD, HEAD)
                value_at = pl.multiple_of(shard.shape[1] // 2 + head * HEAD, HEAD)
                pltpu.sync_copy(shard.at[:, pl.ds(key_at, HEAD)], k_buf.at[here, :])
                pltpu.sync_copy(shard.at[:, pl.ds(value_at, HEAD)], v_buf.at[here, :])
                limit = usable(text_count[0], marks_all[i])

                @pl.loop(0, rows_here // sub)
                def _(n):
                    part = pl.ds(pl.multiple_of(n * sub, sub), sub)
                    scores = score(q_buf[part, :], k_buf[here, :])
                    key = lax.broadcasted_iota(jnp.int32, scores.shape, 1)
                    scores = jnp.where(key < limit, scores, -1e30)
                    old = top_ref[part, :]
                    new = jnp.maximum(old, jnp.max(scores, axis=1, keepdims=True))
                    p = jnp.exp2(scores - new[:, 0:1]).astype(bf16)
                    v = v_buf[here, :]
                    v = jnp.concatenate([v, jnp.ones_like(v)], axis=1)
                    added = jnp.dot(p, v, preferred_element_type=f32)
                    factor = jnp.exp2(old - new)
                    acc_ref[part, :] = acc_ref[part, :] * jnp.concatenate([factor, factor], axis=1) + added
                    top_ref[part, :] = new

            write(as_row(acc_ref, HEAD), as_row(top_ref, 0))


def attend(text_count, queries, shards, acc, everything=None, sub=SUB):
    shards, marks = [kv for kv, _ in shards], [mark for _, mark in shards]
    first, last = acc is None, everything is not None
    marks_all = None
    pieces = len(queries)
    rows = pieces * queries[0].shape[0]
    heads = queries[0].shape[1] // HEAD
    acc_block = pl.BlockSpec((None, rows, 2 * HEAD), lambda h: (h, 0, 0))
    in_specs = [pl.BlockSpec(memory_space=pltpu.SMEM)]
    in_specs += [pl.BlockSpec((q.shape[0], HEAD), lambda h: (0, h)) for q in queries]
    args = [text_count] + list(queries)
    for shift in (0, heads):
        for kv in shards:
            in_specs.append(pl.BlockSpec((kv.shape[0], HEAD), lambda h, s=shift: (0, s + h)))
            args.append(kv)
    if not first:
        in_specs.append(acc_block)
        args.append(acc)
    total = sum(kv.shape[0] for kv in shards)
    scratch = [pltpu.VMEM((total, HEAD), bf16)]
    if last:
        in_specs += [pl.BlockSpec(memory_space=pl.ANY)] * len(everything)
        args += [kv for kv, _ in everything]
        marks_all = [mark for _, mark in everything]
        half = rows // 2
        out_specs = [pl.BlockSpec((half, HEAD), lambda h: (0, h))] * 2
        out_specs += [pl.BlockSpec((None, 2, half), lambda h: (h, 0, 0))] * 2
        out_shape = [jax.ShapeDtypeStruct((half, heads * HEAD), bf16)] * 2
        out_shape += [jax.ShapeDtypeStruct((heads, 2, half), f32)] * 2
        keys = everything[0][0].shape[0]
        scratch += [
            pltpu.VMEM((rows, 2 * HEAD), f32),
            pltpu.VMEM((keys, HEAD), bf16),
            pltpu.VMEM((keys, HEAD), bf16),
            pltpu.VMEM((rows, HEAD), f32),
            pltpu.VMEM((rows, 2 * HEAD), bf16),
        ]
    else:
        out_specs = acc_block
        out_shape = jax.ShapeDtypeStruct((heads, rows, 2 * HEAD), f32)
    return pl.pallas_call(
        functools.partial(attn_kernel, pieces, marks, marks_all, first, last, sub),
        grid=(heads,),
        in_specs=in_specs,
        out_specs=out_specs,
        out_shape=out_shape,
        scratch_shapes=scratch,
        cost_estimate=pl.CostEstimate(
            flops=heads * rows * total * (1 if first else 2048),
            bytes_accessed=(1 if first else 12) * 2**20,
            transcendentals=0 if first else heads * rows * total,
        ),
        compiler_params=pltpu.CompilerParams(vmem_limit_bytes=(50 if last else 58) * 2**20),
    )(*args)


def id_kernel(q_ref, kv_ref, match_ref, out_ref):
    width = q_ref.shape[1]
    match = match_ref[...]
    lacking = 1.0 - jnp.max(match, axis=1, keepdims=True)
    for h in range(width // HEAD):
        cols = slice(h * HEAD, (h + 1) * HEAD)
        scores = lax.dot_general(
            q_ref[:, cols], kv_ref[:, cols], TRANSPOSED, preferred_element_type=f32
        ) * (1.0 / math.sqrt(HEAD))
        scores = jnp.where(match > 0, scores, -1e30)
        peak = jnp.max(scores, axis=1, keepdims=True)
        expo = jnp.exp(scores - peak) * match
        totals = jnp.sum(expo, axis=1, keepdims=True) + lacking
        v = kv_ref[:, width + h * HEAD : width + (h + 1) * HEAD]
        out_ref[:, cols] = jnp.dot(expo.astype(bf16), v, preferred_element_type=f32) / totals


def id_attend(q, id_kv, match):
    return pl.pallas_call(
        id_kernel,
        out_shape=jax.ShapeDtypeStruct(q.shape, f32),
        compiler_params=pltpu.CompilerParams(vmem_limit_bytes=32 * 2**20),
    )(q, id_kv, match)


def combine_kernel(keep, recv, lr_own, lr_core, lr_x, lr_far, id_ref, out_ref):
    slot = pl.program_id(0)
    tokens, width = keep.shape
    place = lax.rem(lax.axis_index("xl") + slot, 2)
    square = (HEAD, HEAD)
    diagonal = lax.broadcasted_iota(jnp.int32, square, 0) == lax.broadcasted_iota(jnp.int32, square, 1)
    for h in range(width // HEAD):
        refs = [r[h, 1:2, :] for r in (lr_own, lr_core, lr_x, lr_far)]
        sums = [r[h, 0:1, :] for r in (lr_own, lr_core, lr_x, lr_far)]
        top = functools.reduce(jnp.maximum, refs)
        weight = [jnp.exp2(r - top) for r in refs]
        total = sum(w * s for w, s in zip(weight, sums))

        scales = [weight[0] / total, weight[1] / total]
        for at in range(0, tokens, HEAD):
            rows, cols = slice(at, at + HEAD), slice(h * HEAD, (h + 1) * HEAD)
            left, right = [], []
            for scale, data in zip(scales, (keep, recv)):
                exact = jnp.where(diagonal, scale[:, rows], 0.0)
                high = exact.astype(bf16)
                left += [high, (exact - high.astype(f32)).astype(bf16)]
                right += [data[rows, cols]] * 2
            value = jnp.dot(
                jnp.concatenate(left, axis=1), jnp.concatenate(right, axis=0), preferred_element_type=f32
            )
            value = value + jnp.where(slot == 0, id_ref[rows, cols], 0.0)
            out_ref[place, rows, cols] = value.astype(bf16)


def combine(keep, recv, lr_keep, lr_core, lr_x, lr_far, idpart):
    tokens, width = idpart.shape
    heads = width // HEAD
    data = pl.BlockSpec((tokens, width), lambda s: (s, 0))
    near = pl.BlockSpec((heads, 2, tokens), lambda s: (0, 0, s))
    cross = pl.BlockSpec((heads, 2, tokens), lambda s: (0, 0, 1 - s))
    return pl.pallas_call(
        combine_kernel,
        grid=(2,),
        in_specs=[data, data, near, near, cross, cross, pl.BlockSpec((tokens, width), lambda s: (0, 0))],
        out_specs=pl.BlockSpec((2, tokens, width), lambda s: (0, 0, 0)),
        out_shape=jax.ShapeDtypeStruct((2, tokens, width), bf16),
        compiler_params=pltpu.CompilerParams(vmem_limit_bytes=16 * 2**20),
    )(keep, recv, lr_keep, lr_core, lr_x, lr_far, idpart)


def normalize(summed, id_gain):
    mean_square = jnp.mean(summed * summed, axis=-1, keepdims=True)
    return (summed * lax.rsqrt(mean_square + 1e-06) * id_gain).astype(bf16)


def pooled_terms(gathered, width):
    return lax.dot_general(
        gathered[:, width:], gathered[:, :width], (((0,), (0,)), ((), ())), preferred_element_type=f32
    )


def identity_rows(pooled, latents, id_gain, id_kv_weight):
    tokens = normalize(latents.astype(f32) + pooled, id_gain)
    return jnp.dot(tokens, id_kv_weight, preferred_element_type=f32).astype(bf16)


def project_kernel(mixed, weight, mine, other, product):
    xh = lax.axis_index("xh")
    groups = weight.shape[0]
    total = None
    for y in range(groups):
        group = (mixed[y].astype(f32) + mixed[groups + y].astype(f32)).astype(bf16)
        part = jnp.dot(group, weight[y], preferred_element_type=f32)
        total = part if total is None else total + part
    product[...] = total
    rows = mine.shape[0]
    mine[...] = product[pl.ds(pl.multiple_of(xh * rows, rows), rows), :]
    other[...] = product[pl.ds(pl.multiple_of((1 - xh) * rows, rows), rows), :].astype(bf16)


def project(mixed, weight):
    tokens, width = mixed.shape[1] // 2, weight.shape[2]
    tile = 512
    columns = pl.BlockSpec(weight.shape[:2] + (tile,), lambda n: (0, 0, n))
    out = pl.BlockSpec((tokens, tile), lambda n: (0, n))
    return pl.pallas_call(
        project_kernel,
        grid=(width // tile,),
        in_specs=[pl.BlockSpec(mixed.shape, lambda n: (0, 0, 0)), columns],
        out_specs=[out, out],
        out_shape=[
            jax.ShapeDtypeStruct((tokens, width), f32),
            jax.ShapeDtypeStruct((tokens, width), bf16),
        ],
        scratch_shapes=[pltpu.VMEM((2 * tokens, tile), f32)],
        cost_estimate=pl.CostEstimate(flops=2 * 10**9, bytes_accessed=10 * 2**20, transcendentals=0),
        compiler_params=pltpu.CompilerParams(vmem_limit_bytes=16 * 2**20),
    )(mixed, weight)


def on_device(
    joint_qkv,
    text_count,
    region_ids,
    region_identity,
    id_feats,
    resample_mix,
    latents,
    id_gain,
    id_kv_weight,
    out_weight,
):
    z_size = lax.axis_size("z")
    y_size = lax.axis_size("y")
    uly = y_size * lax.axis_size("xh")
    tok_dev = joint_qkv.shape[0]
    tok_blk = tok_dev * uly
    width = joint_qkv.shape[2]
    here = width // uly
    my_xl, my_z, my_c = lax.axis_index("xl"), lax.axis_index("z"), lax.axis_index("c")
    number = lax.axis_index(ULY)

    block = (my_xl * z_size + my_z) * 2 + my_c
    lanes = jnp.arange(SUBJ * IDTOK, dtype=jnp.int32) // IDTOK
    own_lanes = lanes[None, None, :] == jnp.arange(SUBJ, dtype=jnp.int32)[:, None, None]
    mix_rows = jnp.where(own_lanes, jnp.tile(resample_mix.T, (1, SUBJ))[None], 0)
    packed = jnp.concatenate([id_feats, mix_rows], axis=2)
    gathered = lax.all_gather(packed, "z", axis=0).reshape(-1, width + SUBJ * IDTOK)

    by_group = joint_qkv.reshape(tok_dev, 3, uly, here)
    position = block * tok_blk + number * tok_dev + jnp.arange(tok_dev, dtype=jnp.int32)
    used = (position >= TXT) | (position < text_count[0])
    values = jnp.where(used[:, None, None], by_group[:, 2], 0)
    sent = jnp.concatenate([by_group[:, 0], by_group[:, 1], values], axis=-1).transpose(1, 0, 2)
    got = lax.all_to_all(sent, ULY, 0, 0, tiled=True).reshape(tok_blk, 3 * here)

    position = block * tok_blk + jnp.arange(tok_blk, dtype=jnp.int32)
    has_id = (region_ids > 0) & (position >= TXT)
    subject = jnp.zeros((tok_blk,), jnp.int32)
    for which in range(SUBJ):
        subject = subject + jnp.where(region_ids == which + 1, region_identity[which], 0)
    key_subject = jnp.arange(SUBJ * IDTOK, dtype=jnp.int32) // IDTOK
    match = ((key_subject[None, :] == subject[:, None]) & has_id[:, None]).astype(f32)
    flat_weight = id_kv_weight.reshape(width, 2 * here)
    half_weight = jnp.where(my_c == 0, out_weight[:, : width // 2], out_weight[:, width // 2 :])
    got, match, flat_weight, half_weight = lax.optimization_barrier((got, match, flat_weight, half_weight))
    weight = lax.all_gather(half_weight, "y", axis=0)
    q_own, kv = lax.optimization_barrier((got[:, :here], got[:, here:]))
    q_x = lax.ppermute(q_own, "xl", SWAP)
    queries = [q_own, q_x, lax.ppermute(q_own, "c", SWAP), lax.ppermute(q_x, "c", SWAP)]

    right = [(i, (i + 1) % z_size) for i in range(z_size)]
    left = [(i, (i - 1) % z_size) for i in range(z_size)]
    half = tok_blk // 2
    end = z_size // 2
    first = (kv, (0, 0, tok_blk))
    up, down, acc = kv, kv, None
    pending = [first]
    whole = []
    for step in range(1, end + 1):
        if step < end:
            up, down = lax.ppermute(up, "z", right), lax.ppermute(down, "z", left)
            arriving = [(up, (step, 0, tok_blk)), (down, (z_size - step, 0, tok_blk))]
        else:
            up, down = lax.ppermute(up[:half], "z", right), lax.ppermute(down[half:], "z", left)
            arriving = [(up, (end, 0, half)), (down, (end, half, half))]
        acc = attend(text_count, queries, pending, acc)
        if step == 1:
            up, down, acc = lax.optimization_barrier((up, down, acc))
        elif step == 2:
            acc, gathered = lax.optimization_barrier((acc, gathered))
            terms = pooled_terms(gathered, width).reshape(2, 2, IDTOK, width)
            own = jnp.where(my_c == 0, terms[:, 0], terms[:, 1])
            other = jnp.where(my_c == 0, terms[:, 1], terms[:, 0])
            up, down, acc, own, other = lax.optimization_barrier((up, down, acc, own, other))
            terms = own + lax.ppermute(other, "c", SWAP)
            pooled = jnp.where(my_xl == 0, terms[0], terms[1])
            pooled = pooled + lax.ppermute(jnp.where(my_xl == 0, terms[1], terms[0]), "xl", SWAP)
        elif step == end - 1:
            id_rows = identity_rows(pooled, latents, id_gain, flat_weight)
            up, down, acc, id_rows = lax.optimization_barrier((up, down, acc, id_rows))
        if step < end:
            arriving = [(up, arriving[0][1]), (down, arriving[1][1])]
        whole += pending
        pending = arriving
    whole += pending
    id_core = lax.ppermute(id_rows, "c", SWAP)
    id_pair = jnp.where(my_c == 0, jnp.stack([id_rows, id_core]), jnp.stack([id_core, id_rows]))
    id_pair, acc = lax.optimization_barrier((id_pair, acc))
    id_x = lax.ppermute(id_pair, "xl", SWAP)
    id_kv = jnp.where(my_xl == 0, jnp.stack([id_pair, id_x]), jnp.stack([id_x, id_pair]))
    id_kv = id_kv.reshape(SUBJ * IDTOK, 2 * here)
    idpart = id_attend(q_own, id_kv, match)
    keep, send, lr_keep, lr_send = attend(text_count, queries, pending, acc, everything=whole)

    recv = lax.ppermute(send, "c", SWAP)
    lr_core = lax.ppermute(lr_send, "c", SWAP)
    lr_x = lax.ppermute(lr_keep, "xl", SWAP)
    lr_far = lax.ppermute(lr_send, ("xl", "c"), [(i, 3 - i) for i in range(4)])
    weight, recv, lr_core, lr_x, lr_far, idpart = lax.optimization_barrier(
        (weight, recv, lr_core, lr_x, lr_far, idpart)
    )
    other_weight = lax.ppermute(weight, "c", SWAP)
    mixed = combine(keep, recv, lr_keep, lr_core, lr_x, lr_far, idpart)

    quarter = tok_blk // y_size
    mixed = mixed.reshape(2 * y_size, quarter, here)
    weight, mixed = lax.optimization_barrier((weight, mixed))
    mixed = lax.all_to_all(mixed, ("xl", "y"), 0, 0, tiled=True)
    out = []
    for columns in (weight, other_weight):
        mine, other = project(mixed, columns)
        out.append((mine + lax.ppermute(other, "xh", SWAP).astype(f32)).astype(bf16))
    low = jnp.where(my_c == 0, out[0], out[1])
    high = jnp.where(my_c == 0, out[1], out[0])
    return jnp.concatenate([low, high], axis=1)


def solution(mesh):
    fine = Mesh(mesh.devices.reshape(2, 8, 2, 4, 2), BLK + ULY)
    placed = (
        P(BLK + ULY, None, None),
        P(),
        P(BLK),
        P(),
        P(None, BLK, None),
        P(None, BLK),
        P(),
        P(),
        P(None, None, ULY),
        P(ULY, None),
    )
    return jax.shard_map(
        on_device, mesh=fine, in_specs=placed, out_specs=P(BLK + ULY, None), check_vma=False
    )
```
